32 devices in a mesh: mem: 8 (over z, y), dp: 4 (over x, core).
Axes of the slice: x: 2, y: 2, z: 4, core: 2. Of those that a mesh axis runs over, the one named last changes fastest.
Arguments:
- grad_out: bfloat16 [16384, 4096], P(('mem', 'dp')), may hold values from -6 to 6
- scores: float32 [16384, 2], P(('mem', 'dp')), may hold values from -4 to 4
- row_ids: int32 [16384, 2], P(('mem', 'dp')), may hold values from 0 to 8191, as said below
- proj_ids: int32 [16384, 2], P(('mem', 'dp')), may hold values from 0 to 1
- values: bfloat16 [8192, 1024], P('mem'), may hold values from -0.1875 to 0.1875
- proj_w: bfloat16 [2, 1024, 4096], P(None, None, 'mem'), may hold values from -0.09375 to 0.09375
Outputs:
- score_grads: float32 [16384, 2], P(('mem', 'dp'))
- value_grads: bfloat16 [8192, 1024], P(('mem', 'dp'))
- proj_grads: float32 [2, 1024, 4096], P(None, 'dp', 'mem')
The draws below stay inside these ranges and needn't reach their ends.
Inputs may be any that keep to these rules, and one draw needn't show every extreme that they name: `row_ids`: row 1024 * o + r lies on index o along mem. Of the 1024 selections of one device at most 256 name rows of one index along mem; among the devices that share one index along dp, one index along mem receives exactly 256 selections from every one of them.
All inputs are finite; a program needn't handle non-finite values.
Results may differ from the reference program's by a relative error of at most 0.012.
Values may be sent and summed in bfloat16 or wider, within the bound.
No kernel may reach another device: no remote copies, remote signals or barrier semaphores. Data moves between devices by JAX's collectives and lax.ppermute only.
A program may use at most 128 MiB of HBM per device.

```python
import jax
import jax.numpy as jnp
from jax import lax

D = 4096
VW = 1024
NPROJ = 2
SEL = 2
TOK_DEV = 512
ROWS_DEV = 1024
TOKENS = 16384
ROWS = 8192
N_MEM = 8
N_DP = 4


def draw_row_ids(key, part):
    blocks = N_MEM * N_DP
    sel_count = TOK_DEV * SEL
    capacity = 2 * sel_count // N_MEM
    others = N_MEM - 1
    hot_owner = jax.random.randint(jax.random.fold_in(key, 11), (N_DP,), 0, N_MEM)

    def one_block(block):
        block_key = jax.random.fold_in(jax.random.fold_in(key, 23), block)
        key_order, key_bits, key_slots, key_rows = jax.random.split(block_key, 4)
        hot = hot_owner[block % N_DP]
        owner_range = jnp.arange(N_MEM, dtype=jnp.int32)
        ranking = jax.random.randint(key_order, (N_MEM,), 0, 1 << 20) * N_MEM + owner_range
        ranking = jnp.where(owner_range == hot, -1, ranking)
        order = jnp.argsort(ranking, stable=True).astype(jnp.int32)
        position = jnp.arange(sel_count, dtype=jnp.int32)
        later = jnp.maximum(position - capacity, 0)
        klass = later % others
        shift_bit = jax.random.randint(key_bits, (sel_count,), 0, 2)
        other_owner = order[1 + (klass + shift_bit) % others]
        owner = jnp.where(position < capacity, hot, other_owner)
        shuffle = jax.random.permutation(key_slots, sel_count)
        owner = owner[shuffle]
        local_row = jax.random.randint(key_rows, (sel_count,), 0, ROWS_DEV)
        return (owner * ROWS_DEV + local_row).astype(jnp.int32)
    every = jax.vmap(one_block)(jnp.arange(blocks, dtype=jnp.int32))
    return every.reshape(blocks * TOK_DEV, SEL)


def plant(result, rng, low, top_value):
    place = [jax.random.randint(jax.random.fold_in(rng, axis), (), 0, length) for axis, length in enumerate(result.shape)]
    widest = result.shape.index(max(result.shape))
    beside = place[:widest] + [(place[widest] + 1) % result.shape[widest]] + place[widest + 1:]
    return result.at[tuple(place)].set(low).at[tuple(beside)].set(top_value)


def block_levels(rng, dims, cuts, smallest, high):
    level, own = 1.0, jax.random.fold_in(rng, 6)
    for axis_at, blocks in cuts:
        draws = jnp.exp(jax.random.uniform(jax.random.fold_in(own, axis_at), (blocks,), jnp.float32, smallest / len(cuts), high / len(cuts)))
        level = level * jnp.repeat(draws, dims[axis_at] // blocks).reshape([-1 if axis == axis_at else 1 for axis in range(len(dims))])
    return level


def bell_draw(rng, extent, deviation, reach, cuts=(), held_as=jnp.bfloat16):
    values = deviation * jax.random.normal(rng, extent, jnp.float32)
    if cuts:
        values = values * block_levels(rng, extent, cuts, -0.22, 0.18)
    return jnp.clip(values, -reach, reach).astype(held_as)


def setup_inputs(seed: int = 0) -> dict:
    streams_of = jax.random.split(jax.random.key(seed), 7)
    grad_out = bell_draw(streams_of[0], (TOKENS, D), 1.0, 6.0, ((0, 32),))
    scores = bell_draw(streams_of[1], (TOKENS, SEL), 1.0, 4.0, ((0, 32),), jnp.float32)
    row_ids = draw_row_ids(jax.random.fold_in(streams_of[6], 71), 0)
    proj_ids = plant(jax.random.randint(streams_of[3], (TOKENS, SEL), 0, NPROJ), jax.random.fold_in(streams_of[3], 1), 0, NPROJ - 1).astype(jnp.int32)
    values = bell_draw(streams_of[4], (ROWS, VW), VW ** -0.5, 0.1875, ((0, 8),))
    proj_w = bell_draw(streams_of[5], (NPROJ, VW, D), D ** -0.5, 0.09375, ((2, 8),))
    return {"grad_out": grad_out, "scores": scores, "row_ids": row_ids, "proj_ids": proj_ids, "values": values, "proj_w": proj_w}


def reference(grad_out, scores, row_ids, proj_ids, values, proj_w):
    token_total = grad_out.shape[0]
    picked = jnp.zeros((token_total, SEL, VW), jnp.float32)
    for which in range(NPROJ):
        projected = jnp.dot(grad_out, proj_w[which].T, preferred_element_type=jnp.float32)
        picked = picked + jnp.where((proj_ids == which)[:, :, None], projected[:, None, :], 0.0)
    contrib = (scores[:, :, None] * picked).astype(jnp.bfloat16)
    flat_rows = row_ids.reshape(-1)
    value_grads = jnp.zeros((ROWS, VW), jnp.float32).at[flat_rows].add(contrib.reshape(-1, VW).astype(jnp.float32))
    value_grads = value_grads.astype(jnp.bfloat16)
    chosen = jnp.take(values, flat_rows, axis=0).reshape(token_total, SEL, VW)
    chosen_wide = chosen.astype(jnp.float32)
    score_grads = jnp.sum(picked * chosen_wide, axis=2)
    mix_list = []
    for which in range(NPROJ):
        weight = jnp.where(proj_ids == which, scores, 0.0)
        mix_list.append(jnp.sum(weight[:, :, None] * chosen_wide, axis=1).astype(jnp.bfloat16))
    mixes = jnp.stack(mix_list, axis=0)
    blocks = N_MEM * N_DP
    mix_blocks = mixes.reshape(NPROJ, blocks, TOK_DEV, VW).transpose(1, 0, 2, 3)
    grad_blocks = grad_out.reshape(blocks, TOK_DEV, D)

    def add_block(carry, pair):
        mix_block, grad_block = pair
        term = jnp.einsum('ptv,td->pvd', mix_block.astype(jnp.float32), grad_block.astype(jnp.float32))
        term = lax.optimization_barrier(term.astype(jnp.bfloat16))
        return carry + term.astype(jnp.float32), None

    proj_grads, unused = lax.scan(add_block, jnp.zeros((NPROJ, VW, D), jnp.float32), (mix_blocks, grad_blocks))
    return score_grads, value_grads, proj_grads
```

```python
import functools

import jax
import jax.numpy as jnp
from jax import lax
from jax.experimental import pallas as pl
from jax.experimental.pallas import tpu as pltpu
from jax.sharding import PartitionSpec as P

F32 = jnp.float32
BF16 = jnp.bfloat16
VMEM_LIMIT = 48 * 1024 * 1024


def params():
    return pltpu.CompilerParams(vmem_limit_bytes=VMEM_LIMIT)


def whole_block(shape):
    return pl.BlockSpec(shape, lambda *_: (0,) * len(shape))


def fetch_kernel(per_token, proj_count, blocks, ids_ref, proj_ref, score_ref, *refs):
    tables, (chosen_ref, mix_ref) = refs[:blocks], refs[blocks:]
    rows, width = tables[0].shape
    tile = ids_ref.shape[0]
    lane = lax.broadcasted_iota(jnp.int32, (tile, rows), 1)
    mixes = [jnp.zeros((tile, width), F32) for _ in range(proj_count)]
    for s in range(per_token):
        ids = ids_ref[:, s : s + 1]
        total = jnp.zeros((tile, width), F32)
        for b in range(blocks):
            hot = jnp.where(lane == ids - b * rows, 1.0, 0.0).astype(BF16)
            total += jnp.dot(hot, tables[b][...], preferred_element_type=F32)
        chosen_ref[s] = total.astype(BF16)
        for j in range(proj_count):
            weight = jnp.where(proj_ref[:, s : s + 1] == j, score_ref[:, s : s + 1], 0.0)
            mixes[j] += weight * total
    mix_ref[...] = jnp.concatenate(mixes, axis=1).astype(BF16).T


def fetch(ids, proj, scores, tables, proj_count):
    tokens, per_token = ids.shape
    rows, width = tables[0].shape
    blocks = len(tables)
    tile = 256
    column = pl.BlockSpec((tile, per_token), lambda i: (i, 0))
    return pl.pallas_call(
        functools.partial(fetch_kernel, per_token, proj_count, blocks),
        grid=(tokens // tile,),
        in_specs=[column] * 3 + [whole_block((rows, width))] * blocks,
        out_specs=[
            pl.BlockSpec((per_token, tile, width), lambda i: (0, i, 0)),
            pl.BlockSpec((proj_count * width, tile), lambda i: (0, i)),
        ],
        out_shape=[
            jax.ShapeDtypeStruct((per_token, tokens, width), BF16),
            jax.ShapeDtypeStruct((proj_count * width, tokens), BF16),
        ],
        compiler_params=params(),
        cost_estimate=pl.CostEstimate(
            flops=2 * tokens * per_token * rows * blocks * width,
            bytes_accessed=2 * rows * blocks * width,
            transcendentals=0,
        ),
        name="fetch",
    )(ids, proj, scores, *tables)


def part_kernel(groups, mix_ref, *refs):
    grads, out_ref = refs[:groups], refs[groups]
    tokens = grads[0].shape[0]
    total = jnp.zeros(out_ref.shape, F32)
    for g in range(groups):
        total += jnp.dot(
            mix_ref[:, g * tokens : (g + 1) * tokens], grads[g][...], preferred_element_type=F32
        )
    out_ref[...] = total.astype(BF16)


def part(mixes, grads):
    depth, tokens = mixes.shape
    rows, columns = grads[0].shape
    tile = 256
    return pl.pallas_call(
        functools.partial(part_kernel, len(grads)),
        grid=(columns // tile,),
        in_specs=[whole_block((depth, tokens))]
        + [pl.BlockSpec((rows, tile), lambda i: (0, i))] * len(grads),
        out_specs=pl.BlockSpec((depth, tile), lambda i: (0, i)),
        out_shape=jax.ShapeDtypeStruct((depth, columns), BF16),
        compiler_params=params(),
        cost_estimate=pl.CostEstimate(
            flops=2 * depth * tokens * columns,
            bytes_accessed=2 * (depth * tokens + tokens * columns + depth * columns),
            transcendentals=0,
        ),
        name="part",
    )(mixes, *grads)


def project_kernel(per_token, nz, ny, proj_ref, score_ref, chosen_ref, *refs):
    grads, weights = refs[:nz], refs[nz : nz + nz * ny]
    contrib_ref, sums_ref = refs[nz + nz * ny :]
    proj_count, width, depth = weights[0].shape
    tile = proj_ref.shape[0]
    contract = (((1,), (1,)), ((), ()))
    projected = [jnp.zeros((tile, width), F32) for _ in range(proj_count)]
    for kz in range(nz):
        for ky in range(ny):
            block = grads[kz][:, ky * depth : (ky + 1) * depth]
            for j in range(proj_count):
                projected[j] += lax.dot_general(
                    block, weights[kz * ny + ky][j], contract, preferred_element_type=F32
                )
    for s in range(per_token):
        picked = jnp.zeros((tile, width), F32)
        for j in range(proj_count):
            picked = jnp.where(proj_ref[:, s : s + 1] == j, projected[j], picked)
        contrib_ref[s] = (score_ref[:, s : s + 1] * picked).astype(BF16)
        sums_ref[:, s : s + 1] = jnp.sum(
            picked * chosen_ref[s].astype(F32), axis=1, keepdims=True
        )


def project(group, proj, scores, chosen, grads, weights):
    per_token, _, width = chosen.shape
    tokens, columns = grads[0].shape
    nz = len(grads)
    ny = len(weights) // nz
    tile = 256
    steps = tokens // tile
    column = pl.BlockSpec((tile, per_token), lambda i: (group * steps + i, 0))
    return pl.pallas_call(
        functools.partial(project_kernel, per_token, nz, ny),
        grid=(steps,),
        in_specs=[
            column,
            column,
            pl.BlockSpec((per_token, tile, width), lambda i: (0, group * steps + i, 0)),
        ]
        + [pl.BlockSpec((tile, columns), lambda i: (i, 0))] * nz
        + [whole_block(weights[0].shape)] * len(weights),
        out_specs=[
            pl.BlockSpec((per_token, tile, width), lambda i: (0, i, 0)),
            pl.BlockSpec((tile, per_token), lambda i: (i, 0)),
        ],
        out_shape=[
            jax.ShapeDtypeStruct((per_token, tokens, width), BF16),
            jax.ShapeDtypeStruct((tokens, per_token), F32),
        ],
        compiler_params=params(),
        cost_estimate=pl.CostEstimate(
            flops=2 * tokens * columns * nz * width * weights[0].shape[0],
            bytes_accessed=2 * tokens * columns * nz,
            transcendentals=0,
        ),
        name="project",
    )(proj, scores, chosen, *grads, *weights)


def scatter_kernel(first, per_token, groups, ids_ref, *refs):
    contribs, out_ref = refs[:groups], refs[groups]
    tile, width = out_ref.shape
    tokens = contribs[0].shape[1]
    base = first + pl.program_id(0) * tile
    row = base + lax.broadcasted_iota(jnp.int32, (tile, tokens), 0)
    total = jnp.zeros((tile, width), F32)
    for g in range(groups):
        for s in range(per_token):
            ids = ids_ref[s : s + 1, g * tokens : (g + 1) * tokens]
            hot = jnp.where(row == ids, 1.0, 0.0).astype(BF16)
            total += jnp.dot(hot, contribs[g][s], preferred_element_type=F32)
    out_ref[...] = total.astype(BF16)


def scatter(first, rows, ids, contribs):
    per_token, tokens, width = contribs[0].shape
    tile = 512
    return pl.pallas_call(
        functools.partial(scatter_kernel, first, per_token, len(contribs)),
        grid=(rows // tile,),
        in_specs=[whole_block(ids.shape)] + [whole_block(contribs[0].shape)] * len(contribs),
        out_specs=pl.BlockSpec((tile, width), lambda i: (i, 0)),
        out_shape=jax.ShapeDtypeStruct((rows, width), BF16),
        compiler_params=params(),
        cost_estimate=pl.CostEstimate(
            flops=2 * rows * per_token * tokens * len(contribs) * width,
            bytes_accessed=2 * per_token * tokens * len(contribs) * width,
            transcendentals=0,
        ),
        name="scatter",
    )(ids, *contribs)


def inner_factor(count):
    inner = 1
    while count % (inner * inner * 4) == 0:
        inner *= 2
    return inner


def local(grad_out, scores, row_ids, proj_ids, values, proj_w):
    mem_size, dp_size = lax.axis_size("mem"), lax.axis_size("dp")
    ny = inner_factor(mem_size)
    nz = mem_size // ny
    nc = 2 if dp_size % 2 == 0 else 1
    nx = dp_size // nc
    mem, dp = lax.axis_index("mem"), lax.axis_index("dp")
    z, y, x, c = mem // ny, mem % ny, dp // nc, dp % nc
    tokens_dev, per_token = scores.shape
    rows_local, value_width = values.shape
    proj_count, _, columns = proj_w.shape
    width = value_width // dp_size

    def turn_mem(a, dz, dy):
        if dz % nz == 0 and dy % ny == 0:
            return a
        pairs = [
            (i * ny + j, ((i + dz) % nz) * ny + (j + dy) % ny)
            for i in range(nz)
            for j in range(ny)
        ]
        return lax.ppermute(a, "mem", pairs)

    def turn_dp(a, dx, dc):
        if dx % nx == 0 and dc % nc == 0:
            return a
        pairs = [
            (i * nc + j, ((i + dx) % nx) * nc + (j + dc) % nc)
            for i in range(nx)
            for j in range(nc)
        ]
        return lax.ppermute(a, "dp", pairs)

    def gather_mem(a):
        out = []
        for kz in range(nz):
            line = turn_mem(a, kz, 0)
            out += [turn_mem(line, 0, ky) for ky in range(ny)]
        return out

    def reduce_mem(pieces):
        total = None
        for kz in range(nz):
            line = pieces[kz][0]
            if ny > 1:
                line = line.astype(F32)
                for ky in range(1, ny):
                    line = line + turn_mem(pieces[kz][ky], 0, -ky).astype(F32)
                line = line.astype(BF16)
            line = turn_mem(line, -kz, 0).astype(F32)
            total = line if total is None else total + line
        return total

    meta = jnp.concatenate(
        [row_ids.astype(F32), proj_ids.astype(F32), scores], axis=1
    )
    meta = jnp.concatenate(
        [turn_dp(meta, kx, kc) for kx in range(nx) for kc in range(nc)], axis=0
    )
    all_rows = meta[:, :per_token].astype(jnp.int32)
    all_proj = meta[:, per_token : 2 * per_token].astype(jnp.int32)
    all_scores = meta[:, 2 * per_token :]
    owner = all_rows // rows_local
    turn = ((z - owner // ny) % nz) * ny + (y - owner % ny) % ny
    ids = turn * rows_local + all_rows % rows_local

    tables = gather_mem(lax.dynamic_slice_in_dim(values, dp * width, width, axis=1))
    grads = []
    for kz in range(nz):
        own = jnp.concatenate(
            [
                lax.dynamic_slice_in_dim(
                    grad_out,
                    (((z - kz) % nz) * ny + (y - ky) % ny) * columns,
                    columns,
                    axis=1,
                )
                for ky in range(ny)
            ],
            axis=1,
        )
        row = []
        for kx in range(nx):
            line = turn_dp(own, kx, 0)
            row += [turn_dp(line, 0, kc) for kc in range(nc)]
        grads.append(row)
    weights = gather_mem(lax.dynamic_slice_in_dim(proj_w, dp * width, width, axis=1))

    chosen, mixes = fetch(ids, all_proj, all_scores, tables, proj_count)

    parts = []
    for kz in range(nz):
        term = part(mixes, grads[kz])
        parts.append([term[:, ky * columns : (ky + 1) * columns] for ky in range(ny)])
    proj_grads = reduce_mem(parts).reshape(proj_count, width, columns)

    contribs, sums = [], []
    for g in range(dp_size):
        contrib, sum_ = project(
            g, all_proj, all_scores, chosen, [grads[kz][g] for kz in range(nz)], weights
        )
        contribs.append(contrib)
        sums.append(sum_)

    score_grads = None
    for g in range(dp_size):
        back = turn_dp(sums[g], -(g // nc), -(g % nc))
        score_grads = back if score_grads is None else score_grads + back

    ids_across = ids.T
    terms = []
    for kz in range(nz):
        span = ny * rows_local
        term = scatter(kz * span, span, ids_across, contribs)
        terms.append([term[ky * rows_local : (ky + 1) * rows_local] for ky in range(ny)])
    mine = reduce_mem(terms).astype(BF16)
    share = rows_local // dp_size
    value_grads = jnp.zeros((share, value_width), BF16)
    for kx in range(nx):
        for kc in range(nc):
            to = ((x + kx) % nx) * nc + (c + kc) % nc
            came = ((x - kx) % nx) * nc + (c - kc) % nc
            piece = turn_dp(
                lax.dynamic_slice_in_dim(mine, to * share, share, axis=0), kx, kc
            )
            value_grads = lax.dynamic_update_slice_in_dim(
                value_grads, piece, came * width, axis=1
            )
    return (score_grads, value_grads, proj_grads)


def solution(mesh):
    return jax.shard_map(
        local,
        mesh=mesh,
        in_specs=(
            P(("mem", "dp"), None),
            P(("mem", "dp"), None),
            P(("mem", "dp"), None),
            P(("mem", "dp"), None),
            P("mem", None),
            P(None, None, "mem"),
        ),
        out_specs=(P(("mem", "dp"), None), P(("mem", "dp"), None), P(None, "dp", "mem")),
        check_vma=False,
    )
```

```python
import functools

import jax
import jax.numpy as jnp
from jax import lax
from jax.experimental import pallas as pl
from jax.experimental.pallas import tpu as pltpu
from jax.sharding import PartitionSpec as P

F32 = jnp.float32
BF16 = jnp.bfloat16
VMEM_LIMIT = 48 * 1024 * 1024


def params():
    return pltpu.CompilerParams(vmem_limit_bytes=VMEM_LIMIT)


def whole_block(shape):
    return pl.BlockSpec(shape, lambda *_: (0,) * len(shape))


def fetch_kernel(per_token, proj_count, blocks, ids_ref, proj_ref, score_ref, *refs):
    tables, (chosen_ref, mix_ref) = refs[:blocks], refs[blocks:]
    rows, width = tables[0].shape
    tile = ids_ref.shape[0]
    lane = lax.broadcasted_iota(jnp.int32, (tile, rows), 1)
    mixes = [jnp.zeros((tile, width), F32) for _ in range(proj_count)]
    for s in range(per_token):
        ids = ids_ref[:, s : s + 1]
        total = jnp.zeros((tile, width), F32)
        for b in range(blocks):
            hot = jnp.where(lane == ids - b * rows, 1.0, 0.0).astype(BF16)
            total += jnp.dot(hot, tables[b][...], preferred_element_type=F32)
        chosen_ref[s] = total.astype(BF16)
        for j in range(proj_count):
            weight = jnp.where(proj_ref[:, s : s + 1] == j, score_ref[:, s : s + 1], 0.0)
            mixes[j] += weight * total
    mix_ref[...] = jnp.concatenate(mixes, axis=1).astype(BF16).T


def fetch(ids, proj, scores, tables, proj_count):
    tokens, per_token = ids.shape
    rows, width = tables[0].shape
    blocks = len(tables)
    tile = 256
    column = pl.BlockSpec((tile, per_token), lambda i: (i, 0))
    return pl.pallas_call(
        functools.partial(fetch_kernel, per_token, proj_count, blocks),
        grid=(tokens // tile,),
        in_specs=[column] * 3 + [whole_block((rows, width))] * blocks,
        out_specs=[
            pl.BlockSpec((per_token, tile, width), lambda i: (0, i, 0)),
            pl.BlockSpec((proj_count * width, tile), lambda i: (0, i)),
        ],
        out_shape=[
            jax.ShapeDtypeStruct((per_token, tokens, width), BF16),
            jax.ShapeDtypeStruct((proj_count * width, tokens), BF16),
        ],
        compiler_params=params(),
        cost_estimate=pl.CostEstimate(
            flops=2 * tokens * per_token * rows * blocks * width,
            bytes_accessed=2 * rows * blocks * width,
            transcendentals=0,
        ),
        name="fetch",
    )(ids, proj, scores, *tables)


def part_kernel(groups, mix_ref, *refs):
    grads, out_ref = refs[:groups], refs[groups]
    tokens = grads[0].shape[0]
    total = jnp.zeros(out_ref.shape, F32)
    for g in range(groups):
        total += jnp.dot(
            mix_ref[:, g * tokens : (g + 1) * tokens], grads[g][...], preferred_element_type=F32
        )
    out_ref[...] = total.astype(BF16)


def part(mixes, grads, first, columns):
    depth, tokens = mixes.shape
    rows = grads[0].shape[0]
    tile = 256
    skip = first // tile
    return pl.pallas_call(
        functools.partial(part_kernel, len(grads)),
        grid=(columns // tile,),
        in_specs=[whole_block((depth, tokens))]
        + [pl.BlockSpec((rows, tile), lambda i: (0, skip + i))] * len(grads),
        out_specs=pl.BlockSpec((depth, tile), lambda i: (0, i)),
        out_shape=jax.ShapeDtypeStruct((depth, columns), BF16),
        compiler_params=params(),
        cost_estimate=pl.CostEstimate(
            flops=2 * depth * tokens * columns,
            bytes_accessed=2 * (depth * tokens + tokens * columns + depth * columns),
            transcendentals=0,
        ),
        name="part",
    )(mixes, *grads)


def project_kernel(per_token, pieces, blocks, proj_ref, score_ref, chosen_ref, *refs):
    grads, weights = refs[:pieces], refs[pieces : pieces + blocks]
    contrib_ref, sums_ref = refs[pieces + blocks :]
    proj_count, width, depth = weights[0].shape
    tile = proj_ref.shape[0]
    contract = (((1,), (1,)), ((), ()))
    projected = [jnp.zeros((tile, width), F32) for _ in range(proj_count)]
    at = 0
    for grad in grads:
        for first in range(0, grad.shape[1], depth):
            block = grad[:, first : first + depth]
            for j in range(proj_count):
                projected[j] += lax.dot_general(
                    block, weights[at][j], contract, preferred_element_type=F32
                )
            at += 1
    for s in range(per_token):
        picked = jnp.zeros((tile, width), F32)
        for j in range(proj_count):
            picked = jnp.where(proj_ref[:, s : s + 1] == j, projected[j], picked)
        contrib_ref[s] = (score_ref[:, s : s + 1] * picked).astype(BF16)
        sums_ref[:, s : s + 1] = jnp.sum(
            picked * chosen_ref[s].astype(F32), axis=1, keepdims=True
        )


def project(group, proj, scores, chosen, grads, weights):
    per_token, _, width = chosen.shape
    tokens = grads[0].shape[0]
    columns = sum(grad.shape[1] for grad in grads)
    tile = 256
    steps = tokens // tile
    column = pl.BlockSpec((tile, per_token), lambda i: (group * steps + i, 0))
    return pl.pallas_call(
        functools.partial(project_kernel, per_token, len(grads), len(weights)),
        grid=(steps,),
        in_specs=[
            column,
            column,
            pl.BlockSpec((per_token, tile, width), lambda i: (0, group * steps + i, 0)),
        ]
        + [pl.BlockSpec((tile, grad.shape[1]), lambda i: (i, 0)) for grad in grads]
        + [whole_block(weights[0].shape)] * len(weights),
        out_specs=[
            pl.BlockSpec((per_token, tile, width), lambda i: (0, i, 0)),
            pl.BlockSpec((tile, per_token), lambda i: (i, 0)),
        ],
        out_shape=[
            jax.ShapeDtypeStruct((per_token, tokens, width), BF16),
            jax.ShapeDtypeStruct((tokens, per_token), F32),
        ],
        compiler_params=params(),
        cost_estimate=pl.CostEstimate(
            flops=2 * tokens * columns * width * weights[0].shape[0],
            bytes_accessed=2 * tokens * columns,
            transcendentals=0,
        ),
        name="project",
    )(proj, scores, chosen, *grads, *weights)


def scatter_kernel(first, per_token, groups, ids_ref, *refs):
    contribs, out_ref = refs[:groups], refs[groups]
    tile, width = out_ref.shape
    tokens = contribs[0].shape[1]
    base = first + pl.program_id(0) * tile
    row = base + lax.broadcasted_iota(jnp.int32, (tile, tokens), 0)
    total = jnp.zeros((tile, width), F32)
    for g in range(groups):
        for s in range(per_token):
            ids = ids_ref[s : s + 1, g * tokens : (g + 1) * tokens]
            hot = jnp.where(row == ids, 1.0, 0.0).astype(BF16)
            total += jnp.dot(hot, contribs[g][s], preferred_element_type=F32)
    out_ref[...] = total.astype(BF16)


def scatter(first, rows, ids, contribs):
    per_token, tokens, width = contribs[0].shape
    tile = 512
    return pl.pallas_call(
        functools.partial(scatter_kernel, first, per_token, len(contribs)),
        grid=(rows // tile,),
        in_specs=[whole_block(ids.shape)] + [whole_block(contribs[0].shape)] * len(contribs),
        out_specs=pl.BlockSpec((tile, width), lambda i: (i, 0)),
        out_shape=jax.ShapeDtypeStruct((rows, width), BF16),
        compiler_params=params(),
        cost_estimate=pl.CostEstimate(
            flops=2 * rows * per_token * tokens * len(contribs) * width,
            bytes_accessed=2 * per_token * tokens * len(contribs) * width,
            transcendentals=0,
        ),
        name="scatter",
    )(ids, *contribs)


def inner_factor(count):
    inner = 1
    while count % (inner * inner * 4) == 0:
        inner *= 2
    return inner


def local(grad_out, scores, row_ids, proj_ids, values, proj_w):
    mem_size, dp_size = lax.axis_size("mem"), lax.axis_size("dp")
    ny = inner_factor(mem_size)
    nz = mem_size // ny
    nc = 2 if dp_size % 2 == 0 else 1
    nx = dp_size // nc
    mem, dp = lax.axis_index("mem"), lax.axis_index("dp")
    z, y, x, c = mem // ny, mem % ny, dp // nc, dp % nc
    tokens_dev, per_token = scores.shape
    rows_local, value_width = values.shape
    proj_count, _, columns = proj_w.shape
    width = value_width // dp_size

    last = {}

    def send(a, axis, pairs, lane):
        if lane in last:
            a, last[lane] = lax.optimization_barrier((a, last[lane]))
        last[lane] = lax.ppermute(a, axis, pairs)
        return last[lane]

    def turn_mem(a, dz, dy, lane):
        if dz % nz == 0 and dy % ny == 0:
            return a
        pairs = [
            (i * ny + j, ((i + dz) % nz) * ny + (j + dy) % ny)
            for i in range(nz)
            for j in range(ny)
        ]
        return send(a, "mem", pairs, lane)

    def turn_dp(a, dx, dc, lane):
        if dx % nx == 0 and dc % nc == 0:
            return a
        pairs = [
            (i * nc + j, ((i + dx) % nx) * nc + (j + dc) % nc)
            for i in range(nx)
            for j in range(nc)
        ]
        return send(a, "dp", pairs, lane)

    def columns_of(kz):
        return [
            lax.dynamic_slice_in_dim(
                grad_out,
                (((z - kz) % nz) * ny + (y - ky) % ny) * columns,
                columns,
                axis=1,
            )
            for ky in range(ny)
        ]

    order = list(range(1, nz)) + [0]
    half = nz // 2
    spans = [order[:half], order[half:]] if half else [order]
    own = [
        jnp.concatenate([part_ for kz in span for part_ in columns_of(kz)], axis=1)
        for span in spans
    ]
    grads = [[None] * dp_size for _ in spans]

    def spread(piece, kx, line):
        for kc in range(nc):
            grads[piece][kx * nc + kc] = turn_dp(line, 0, kc, "core")

    lines = {}
    for kx in range(1, nx):
        for piece in range(len(spans)):
            lines[piece, kx] = turn_dp(own[piece], kx, 0, "x")

    quarter_v = lax.dynamic_slice_in_dim(values, dp * width, width, axis=1)
    quarter_w = lax.dynamic_slice_in_dim(proj_w, dp * width, width, axis=1)
    lanes = [f"y{k}" for k in range(2)]
    turn_count = {"y": 0}

    def y_lane():
        turn_count["y"] += 1
        return lanes[turn_count["y"] % 2]

    tables = [None] * mem_size
    weights = [None] * mem_size

    def fan(into, kz, line):
        for ky in range(ny):
            into[kz * ny + ky] = turn_mem(line, 0, ky, y_lane())

    fan(tables, 0, quarter_v)
    for piece in range(len(spans)):
        spread(piece, 0, own[piece])
    fan(weights, 0, quarter_w)
    v_lines, w_lines = {0: quarter_v}, {0: quarter_w}
    jobs = []
    for into, held in ((tables, v_lines), (weights, w_lines)):
        jobs += [(into, held, kz) for kz in [1, nz - 1] + list(range(2, nz - 1))]
    for at, (into, held, kz) in enumerate(jobs):
        if kz in held:
            continue
        lane = f"z{at % 2}"
        if kz == nz - 1:
            held[kz] = turn_mem(held[0], -1, 0, lane)
        else:
            held[kz] = turn_mem(held[kz - 1], 1, 0, lane)
        fan(into, kz, held[kz])

    meta = jnp.concatenate(
        [row_ids.astype(F32), proj_ids.astype(F32), scores], axis=1
    )
    meta = jnp.concatenate(
        [turn_dp(meta, kx, kc, "core") for kx in range(nx) for kc in range(nc)], axis=0
    )
    all_rows = meta[:, :per_token].astype(jnp.int32)
    all_proj = meta[:, per_token : 2 * per_token].astype(jnp.int32)
    all_scores = meta[:, 2 * per_token :]
    owner = all_rows // rows_local
    turn = ((z - owner // ny) % nz) * ny + (y - owner % ny) % ny
    ids = turn * rows_local + all_rows % rows_local

    for kx in range(1, nx):
        for piece in range(len(spans)):
            spread(piece, kx, lines[piece, kx])

    chosen, mixes = fetch(ids, all_proj, all_scores, tables, proj_count)

    def fold(term, kz, lane):
        line = term[0]
        if ny > 1:
            line = line.astype(F32)
            for ky in range(1, ny):
                line = line + turn_mem(term[ky], 0, -ky, y_lane()).astype(F32)
            line = line.astype(BF16)
        return turn_mem(line, -kz, 0, lane).astype(F32)

    def fold_part(kz):
        piece = next(p for p, span in enumerate(spans) if kz in span)
        at = spans[piece].index(kz) * ny * columns
        term = part(mixes, grads[piece], at, ny * columns)
        return fold(
            [term[:, ky * columns : (ky + 1) * columns] for ky in range(ny)], kz, f"z{kz % 2}"
        )

    w_sum = sum(fold_part(kz) for kz in spans[0])

    contribs, sums = [], []
    depths = [weights[kz * ny + ky] for span in spans for kz in span for ky in range(ny)]
    for g in range(dp_size):
        contrib, sum_ = project(
            g, all_proj, all_scores, chosen, [held[g] for held in grads], depths
        )
        contribs.append(contrib)
        sums.append(sum_)

    ids_across = ids.T
    v_sum = None
    for kz in order:
        span = ny * rows_local
        term = scatter(kz * span, span, ids_across, contribs)
        line = fold(
            [term[ky * rows_local : (ky + 1) * rows_local] for ky in range(ny)], kz, f"z{kz % 2}"
        )
        v_sum = line if v_sum is None else v_sum + line

    for kz in [kz for span in spans[1:] for kz in span]:
        w_sum = w_sum + fold_part(kz)
    proj_grads = w_sum.reshape(proj_count, width, columns)

    score_grads = None
    for g in range(dp_size):
        back = turn_dp(sums[g], -(g // nc), -(g % nc), "core")
        score_grads = back if score_grads is None else score_grads + back

    mine = v_sum.astype(BF16)
    share = rows_local // dp_size
    value_grads = jnp.zeros((share, value_width), BF16)
    for kx in range(nx):
        for kc in range(nc):
            to = ((x + kx) % nx) * nc + (c + kc) % nc
            came = ((x - kx) % nx) * nc + (c - kc) % nc
            piece = turn_dp(
                lax.dynamic_slice_in_dim(mine, to * share, share, axis=0),
                kx,
                kc,
                "x" if kx else "core",
            )
            value_grads = lax.dynamic_update_slice_in_dim(
                value_grads, piece, came * width, axis=1
            )
    return (score_grads, value_grads, proj_grads)


def solution(mesh):
    return jax.shard_map(
        local,
        mesh=mesh,
        in_specs=(
            P(("mem", "dp"), None),
            P(("mem", "dp"), None),
            P(("mem", "dp"), None),
            P(("mem", "dp"), None),
            P("mem", None),
            P(None, None, "mem"),
        ),
        out_specs=(P(("mem", "dp"), None), P(("mem", "dp"), None), P(None, "dp", "mem")),
        check_vma=False,
    )
```

```python
import functools

import jax
import jax.numpy as jnp
from jax import lax
from jax.experimental import pallas as pl
from jax.experimental.pallas import tpu as pltpu
from jax.sharding import PartitionSpec as P

F32 = jnp.float32
BF16 = jnp.bfloat16
VMEM_LIMIT = 60 * 1024 * 1024


def params():
    return pltpu.CompilerParams(vmem_limit_bytes=VMEM_LIMIT)


def whole_block(shape):
    return pl.BlockSpec(shape, lambda *_: (0,) * len(shape))


def copy_kernel(index_ref, in_ref, out_ref):
    out_ref[...] = in_ref[...]


def pick_blocks(index, a, block, axis):
    count = index.shape[0]
    shape = list(a.shape)
    shape[axis] = count * block
    tile = list(a.shape)
    tile[axis] = block

    def at(k):
        return tuple(k if dim == axis else 0 for dim in range(a.ndim))

    return pl.pallas_call(
        copy_kernel,
        grid_spec=pltpu.PrefetchScalarGridSpec(
            num_scalar_prefetch=1,
            grid=(count,),
            in_specs=[pl.BlockSpec(tuple(tile), lambda i, index_ref: at(index_ref[i]))],
            out_specs=pl.BlockSpec(tuple(tile), lambda i, index_ref: at(i)),
        ),
        out_shape=jax.ShapeDtypeStruct(tuple(shape), a.dtype),
        compiler_params=params(),
        name="pick",
    )(index, a)


def share_kernel(index_ref, value_ref, weight_ref, out_ref):
    count, width, depth = weight_ref.shape
    rows = value_ref.shape[0]
    out_ref[:rows] = value_ref[...]
    for j in range(count):
        out_ref[rows + j * depth : rows + (j + 1) * depth] = weight_ref[j].T


def pick_share(index, values, proj_w, width):
    rows = values.shape[0]
    count, _, depth = proj_w.shape
    return pl.pallas_call(
        share_kernel,
        grid_spec=pltpu.PrefetchScalarGridSpec(
            num_scalar_prefetch=1,
            grid=(1,),
            in_specs=[
                pl.BlockSpec((rows, width), lambda i, index_ref: (0, index_ref[0])),
                pl.BlockSpec((count, width, depth), lambda i, index_ref: (0, index_ref[0], 0)),
            ],
            out_specs=pl.BlockSpec((rows + count * depth, width), lambda i, index_ref: (0, 0)),
        ),
        out_shape=jax.ShapeDtypeStruct((rows + count * depth, width), values.dtype),
        compiler_params=params(),
        name="share",
    )(index, values, proj_w)


def fetch_kernel(per_token, proj_count, rows, places, has_total, is_last, meta_ref, *refs):
    if has_total:
        before_ref, refs = refs[0], refs[1:]
    tables, chosen_ref = refs[: len(places)], refs[len(places)]
    width = tables[0].shape[1]
    tile = meta_ref.shape[1]
    meta = meta_ref[...].T
    lane = lax.broadcasted_iota(jnp.int32, (tile, rows), 1)
    mixes = [jnp.zeros((tile, width), F32) for _ in range(proj_count)]
    for s in range(per_token):
        ids = meta[:, s : s + 1].astype(jnp.int32)
        total = jnp.zeros((tile, width), F32)
        for table, blocks in zip(tables, places, strict=True):
            for at, block in enumerate(blocks):
                hot = jnp.where(lane == ids - block * rows, 1.0, 0.0).astype(BF16)
                total += jnp.dot(
                    hot, table[at * rows : (at + 1) * rows], preferred_element_type=F32
                )
        if has_total:
            total += before_ref[s].astype(F32)
        chosen_ref[s] = total.astype(BF16)
        if is_last:
            proj = meta[:, per_token + s : per_token + s + 1]
            score = meta[:, 2 * per_token + s : 2 * per_token + s + 1]
            for j in range(proj_count):
                mixes[j] += jnp.where(proj == j, score, 0.0) * total
    if is_last:
        refs[len(places) + 1][...] = jnp.concatenate(mixes, axis=1).astype(BF16).T


def fetch(meta, per_token, rows, tables, places, before, proj_count, is_last):
    tokens = meta.shape[1]
    width = tables[0].shape[1]
    tile = 512
    picked = pl.BlockSpec((per_token, tile, width), lambda i: (0, i, 0))
    args, specs = [meta], [pl.BlockSpec((meta.shape[0], tile), lambda i: (0, i))]
    if before is not None:
        args.append(before)
        specs.append(picked)
    out_specs = [picked]
    out_shape = [jax.ShapeDtypeStruct((per_token, tokens, width), BF16)]
    if is_last:
        out_specs.append(pl.BlockSpec((proj_count * width, tile), lambda i: (0, i)))
        out_shape.append(jax.ShapeDtypeStruct((proj_count * width, tokens), BF16))
    count = sum(len(blocks) for blocks in places)
    return pl.pallas_call(
        functools.partial(
            fetch_kernel, per_token, proj_count, rows, places, before is not None, is_last
        ),
        grid=(tokens // tile,),
        in_specs=specs
        + [whole_block((len(blocks) * rows, width)) for blocks in places],
        out_specs=out_specs,
        out_shape=out_shape,
        compiler_params=params(),
        cost_estimate=pl.CostEstimate(
            flops=2 * tokens * per_token * rows * count * width,
            bytes_accessed=2 * rows * count * width,
            transcendentals=0,
        ),
        name="fetch",
    )(*args, *tables)


def part_kernel(near, far, count, steps, index_ref, mix_ref, *refs):
    wholes, refs = refs[:near], refs[near:]
    pieces, outs = refs[: far * count], refs[far * count :]
    tokens = wholes[0].shape[0]
    ny = len(outs) // count
    for at in range(count):
        for ky in range(ny):
            place = at * ny + ky

            @pl.when(pl.program_id(0) // steps == place)
            def _(at=at, place=place):
                total = jnp.zeros(outs[0].shape, F32)
                for g, grad in enumerate([*wholes, *pieces[at * far : (at + 1) * far]]):
                    total += jnp.dot(
                        mix_ref[:, g * tokens : (g + 1) * tokens],
                        grad[...],
                        preferred_element_type=F32,
                    )
                outs[place][...] = total.astype(BF16)


def part(index, mixes, wholes, pieces, first, ny, columns):
    depth, tokens = mixes.shape
    rows = wholes[0].shape[0]
    tile = 256
    steps = columns // tile
    count, far = len(pieces), len(pieces[0])

    def whole(i, index_ref):
        return (0, index_ref[first * ny + i // steps] * steps + i % steps)

    def within(low, size):
        return lambda i, index_ref: (0, jnp.clip(i - low, 0, size - 1))

    specs = [pl.BlockSpec((rows, tile), whole)] * len(wholes)
    for at in range(count):
        specs += [pl.BlockSpec((rows, tile), within(at * ny * steps, ny * steps))] * far
    return pl.pallas_call(
        functools.partial(part_kernel, len(wholes), far, count, steps),
        grid_spec=pltpu.PrefetchScalarGridSpec(
            num_scalar_prefetch=1,
            grid=(count * ny * steps,),
            in_specs=[whole_block((depth, tokens))] + specs,
            out_specs=[
                pl.BlockSpec((depth, tile), within(place * steps, steps))
                for place in range(count * ny)
            ],
        ),
        out_shape=[jax.ShapeDtypeStruct((depth, columns), BF16)] * (count * ny),
        compiler_params=params(),
        cost_estimate=pl.CostEstimate(
            flops=2 * depth * tokens * columns * count * ny,
            bytes_accessed=2 * (depth * tokens + (tokens + depth) * columns * count * ny),
            transcendentals=0,
        ),
        name="part",
    )(index, mixes, *wholes, *[a for piece in pieces for a in piece])


def project_kernel(shape, weight_rows, index_ref, meta_ref, chosen_ref, *refs):
    per_token, nz, ny, near, far, proj_count = shape
    wholes, refs = refs[: near * ny], refs[near * ny :]
    pieces, refs = refs[: far * nz], refs[far * nz :]
    weights, refs = refs[: nz * ny], refs[nz * ny :]
    contrib_ref, sums_ref, total, held_pieces, held_weights, sems = refs
    tokens, width = wholes[0].shape[0], chosen_ref.shape[2]
    depth = wholes[0].shape[1]
    step = pl.program_id(0)

    def copies(at):
        slot = at % 2
        out = [
            pltpu.make_async_copy(
                pieces[at * far + g], held_pieces.at[slot, g], sems.at[slot, g]
            )
            for g in range(far)
        ]
        for ky in range(ny):
            low = weight_rows[at * ny + ky]
            out.append(
                pltpu.make_async_copy(
                    weights[at * ny + ky].at[low : low + proj_count * depth],
                    held_weights.at[slot, ky],
                    sems.at[slot, far + ky],
                )
            )
        return out

    for at in range(nz):

        @pl.when(step == at)
        def _(at=at):
            slot = at % 2
            if at == 0:
                for copy in copies(0):
                    copy.start()
            for copy in copies(at):
                copy.wait()
            if at + 1 < nz:
                for copy in copies(at + 1):
                    copy.start()
            weight = [
                jnp.concatenate(
                    [
                        held_weights[slot, ky, j * depth : (j + 1) * depth]
                        for j in range(proj_count)
                    ],
                    axis=1,
                )
                for ky in range(ny)
            ]
            for g in range(near + far):
                span = slice(g * tokens, (g + 1) * tokens)
                term = jnp.zeros((tokens, proj_count * width), F32)
                for ky in range(ny):
                    if g < near:
                        block = wholes[g * ny + ky][...]
                    else:
                        block = held_pieces[slot, g - near, :, ky * depth : (ky + 1) * depth]
                    term += jnp.dot(block, weight[ky], preferred_element_type=F32)
                if at == 0:
                    total[span] = term
                elif at < nz - 1:
                    total[span] += term
                else:
                    projected = total[span] + term
                    meta = meta_ref[:, span].T
                    for s in range(per_token):
                        proj = meta[:, per_token + s : per_token + s + 1]
                        score = meta[:, 2 * per_token + s : 2 * per_token + s + 1]
                        picked = jnp.zeros((tokens, width), F32)
                        for j in range(proj_count):
                            picked = jnp.where(
                                proj == j, projected[:, j * width : (j + 1) * width], picked
                            )
                        contrib_ref[s, span] = (score * picked).astype(BF16)
                        sums_ref[span, s : s + 1] = jnp.sum(
                            picked * chosen_ref[s, span].astype(F32), axis=1, keepdims=True
                        )


def project(index, per_token, meta, chosen, wholes, pieces, weights, weight_rows, proj_count, depth):
    _, total, width = chosen.shape
    nz, far, near = len(pieces), len(pieces[0]), len(wholes)
    ny = len(weights) // nz
    tokens = wholes[0].shape[0]
    specs = []
    for _ in range(near):
        for ky in range(ny):
            specs.append(
                pl.BlockSpec(
                    (tokens, depth),
                    lambda i, index_ref, ky=ky: (0, index_ref[i * ny + ky]),
                )
            )
    specs += [pl.BlockSpec(memory_space=pl.ANY)] * (far * nz + len(weights))
    sums_shape = (total, per_token)
    return pl.pallas_call(
        functools.partial(
            project_kernel, (per_token, nz, ny, near, far, proj_count), weight_rows
        ),
        grid_spec=pltpu.PrefetchScalarGridSpec(
            num_scalar_prefetch=1,
            grid=(nz,),
            in_specs=[whole_block(meta.shape), whole_block(chosen.shape)] + specs,
            out_specs=[whole_block(chosen.shape), whole_block(sums_shape)],
            scratch_shapes=[
                pltpu.VMEM((total, proj_count * width), F32),
                pltpu.VMEM((2, max(far, 1), tokens, ny * depth), BF16),
                pltpu.VMEM((2, ny, proj_count * depth, width), BF16),
                pltpu.SemaphoreType.DMA((2, far + ny)),
            ],
        ),
        out_shape=[
            jax.ShapeDtypeStruct(chosen.shape, BF16),
            jax.ShapeDtypeStruct(sums_shape, F32),
        ],
        compiler_params=params(),
        cost_estimate=pl.CostEstimate(
            flops=2 * total * depth * len(weights) * width * proj_count,
            bytes_accessed=2 * total * depth * len(weights),
            transcendentals=0,
        ),
        name="project",
    )(
        index,
        meta,
        chosen,
        *[a for a in wholes for _ in range(ny)],
        *[a for piece in pieces for a in piece],
        *weights,
    )


def scatter_kernel(per_token, sets, steps, meta_ref, contrib_ref, *outs):
    tile, width = outs[0].shape
    tokens = meta_ref.shape[1]
    chunk = 512
    step = pl.program_id(0)
    base, at = jnp.int32(0), 0
    for blocks in sets:
        for block in blocks:
            base = jnp.where(step // steps == at, block * steps * tile, base)
            at += 1
    row = base + (step % steps) * tile + lax.broadcasted_iota(jnp.int32, (tile, chunk), 0)
    total = jnp.zeros((tile, width), F32)
    for first in range(0, tokens, chunk):
        for s in range(per_token):
            ids = meta_ref[s : s + 1, first : first + chunk].astype(jnp.int32)
            hot = jnp.where(row == ids, 1.0, 0.0).astype(BF16)
            total += jnp.dot(
                hot, contrib_ref[s, first : first + chunk], preferred_element_type=F32
            )
    low = 0
    for blocks, out in zip(sets, outs, strict=True):

        @pl.when((step >= low) & (step < low + len(blocks) * steps))
        def _(out=out):
            out[...] = total.astype(BF16)

        low += len(blocks) * steps


def scatter(sets, rows, meta, contrib):
    per_token, tokens, width = contrib.shape
    tile = 512
    steps = rows // tile
    out_specs, low = [], 0
    for blocks in sets:
        size = len(blocks) * steps
        out_specs.append(
            pl.BlockSpec(
                (tile, width), lambda i, low=low, size=size: (jnp.clip(i - low, 0, size - 1), 0)
            )
        )
        low += size
    return pl.pallas_call(
        functools.partial(scatter_kernel, per_token, sets, steps),
        grid=(low,),
        in_specs=[whole_block(meta.shape), whole_block(contrib.shape)],
        out_specs=out_specs,
        out_shape=[
            jax.ShapeDtypeStruct((len(blocks) * rows, width), BF16) for blocks in sets
        ],
        compiler_params=params(),
        cost_estimate=pl.CostEstimate(
            flops=2 * low * tile * per_token * tokens * width,
            bytes_accessed=2 * per_token * tokens * width,
            transcendentals=0,
        ),
        name="scatter",
    )(meta, contrib)


def inner_factor(count):
    inner = 1
    while count % (inner * inner * 4) == 0:
        inner *= 2
    return inner


class Plan:
    def __init__(self, room, work_room):
        self.room, self.work_room = room, work_room
        self.jobs, self.env = [], {}

    def move(self, name, kind, size, needs, operand, axis, pairs):
        self.jobs.append((name, kind, size, needs, operand, axis, pairs))

    def work(self, name, size, needs, run):
        self.jobs.append((name, "work", size, needs, run, None, None))

    def value(self, name, a):
        self.env[name] = a

    def run(self):
        held, env = (), self.env
        while self.jobs:
            ready = set(env)
            moves, works = [], []
            room = dict(self.room)
            for job in self.jobs:
                if job[1] != "work" and set(job[3]) <= ready and job[2] <= room[job[1]]:
                    room[job[1]] -= job[2]
                    moves.append(job)
            ready |= {job[0] for job in moves if job[1] == "core"}
            left = self.work_room
            for job in self.jobs:
                if job[1] == "work" and set(job[3]) <= ready and (job[2] <= left or not works):
                    left -= job[2]
                    ready.add(job[0])
                    works.append(job)
            assert moves or works
            names = set(held) | {n for job in (*moves, *works) for n in job[3] if n in env}
            names = sorted(names)
            if held:
                leaves, tree = jax.tree.flatten([env[n] for n in names])
                passed = jax.tree.unflatten(tree, lax.optimization_barrier(tuple(leaves)))
                env.update(zip(names, passed, strict=True))
            came = [lax.ppermute(job[4](env), job[5], job[6]) for job in moves]
            for a, job in zip(came, moves, strict=True):
                env[job[0]] = a
            for job in works:
                env[job[0]] = job[4](env)
            held = [job[0] for job in (*moves, *works)]
            self.jobs = [job for job in self.jobs if job[0] not in env]
        return env


def local(grad_out, scores, row_ids, proj_ids, values, proj_w):
    mem_size, dp_size = lax.axis_size("mem"), lax.axis_size("dp")
    ny = inner_factor(mem_size)
    nz = mem_size // ny
    nc = 2 if dp_size % 2 == 0 else 1
    nx = dp_size // nc
    mem, dp = lax.axis_index("mem"), lax.axis_index("dp")
    z, y, x, c = mem // ny, mem % ny, dp // nc, dp % nc
    tokens_dev, per_token = scores.shape
    rows_local, value_width = values.shape
    proj_count, _, columns = proj_w.shape
    width = value_width // dp_size

    def mem_pairs(dz, dy):
        return [
            (i * ny + j, ((i + dz) % nz) * ny + (j + dy) % ny)
            for i in range(nz)
            for j in range(ny)
        ]

    def dp_pairs(dx, dc):
        return [
            (i * nc + j, ((i + dx) % nx) * nc + (j + dc) % nc)
            for i in range(nx)
            for j in range(nc)
        ]

    plan = Plan({"y": 2, "z": 2, "x": 2, "core": 8, "small": 8}, 24)
    env = plan.env

    chain = list(range(nz - 2, 0, -1))
    order = chain[:1] + list(range(nz - 1, max(nz - 2, 0), -1)) + chain[1:] + [0]
    kz = jnp.repeat(jnp.array(order, jnp.int32), ny)
    ky = jnp.tile(jnp.arange(ny, dtype=jnp.int32), nz)
    index = ((z - kz) % nz) * ny + (y - ky) % ny

    fields = 3 * per_token
    plan.value(
        "meta0",
        jnp.concatenate(
            [
                row_ids.astype(F32).T,
                proj_ids.astype(F32).T,
                scores.T,
                jnp.zeros((-fields % 8, tokens_dev), F32),
            ],
            axis=0,
        ),
    )
    for g in range(1, dp_size):
        plan.move(
            f"meta{g}", "small", 1, ["meta0"], lambda env: env["meta0"], "dp", dp_pairs(g // nc, g % nc)
        )

    def unpack(env):
        meta = jnp.concatenate([env[f"meta{g}"] for g in range(dp_size)], axis=1)
        all_rows = meta[:per_token].astype(jnp.int32)
        owner = all_rows // rows_local
        turn = ((z - owner // ny) % nz) * ny + (y - owner % ny) % ny
        ids = turn * rows_local + all_rows % rows_local
        return jnp.concatenate([ids.astype(F32), meta[per_token:]], axis=0)

    plan.work("meta", 1, [f"meta{g}" for g in range(dp_size)], unpack)

    plan.value("index", index)
    plan.value("whole0", grad_out)
    plan.value("dp", dp[None].astype(jnp.int32))
    plan.value("values", values)
    plan.value("proj_w", proj_w)
    plan.work(
        "share",
        3,
        ["dp", "values", "proj_w"],
        lambda env: pick_share(env["dp"], env["values"], env["proj_w"], width),
    )
    plan.work("V0", 0, ["share"], lambda env: env["share"][:rows_local])
    plan.work("W0", 0, ["share"], lambda env: env["share"][rows_local:])
    plan.work(
        "own0",
        3,
        ["index", "whole0"],
        lambda env: pick_blocks(env["index"][:ny], env["whole0"], columns, 1),
    )

    hops = ([(1, 0, 1)] if nz > 1 else []) + ([(nz - 1, 0, -1)] if nz > 2 else [])
    hops += [(k, k - 1, 1) for k in range(2, nz - 1)]
    queue = [(kind, *hop) for kind in "VW" for hop in hops]
    place = {("V", 0, 0): ("share", 0), ("W", 0, 0): ("share", rows_local)}
    for dy in range(1, ny):
        plan.move(f"Y0_{dy}", "y", 2, ["share"], lambda env: env["share"], "mem", mem_pairs(0, dy))
        place["V", 0, dy] = (f"Y0_{dy}", 0)
        place["W", 0, dy] = (f"Y0_{dy}", rows_local)
    for kind, k, source, dz in queue:
        plan.move(
            f"{kind}{k}",
            "z",
            1,
            [f"{kind}{source}"],
            lambda env, name=f"{kind}{source}": env[name],
            "mem",
            mem_pairs(dz, 0),
        )
        place[kind, k, 0] = (f"{kind}{k}", 0)
    for first in range(0, len(queue), 2):
        two = queue[first : first + 2]
        names = [f"{kind}{k}" for kind, k, _, _ in two]
        if first + 2 >= len(queue):
            for name, (kind, k, _, _) in zip(names, two, strict=True):
                for dy in range(1, ny):
                    plan.move(
                        f"{name}_{dy}",
                        "y",
                        1,
                        [name],
                        lambda env, name=name: env[name],
                        "mem",
                        mem_pairs(0, dy),
                    )
                    place[kind, k, dy] = (f"{name}_{dy}", 0)
            break
        for dy in range(1, ny):
            plan.move(
                f"Y{first + 1}_{dy}",
                "y",
                2,
                names,
                lambda env, names=names: jnp.concatenate([env[n] for n in names], axis=0),
                "mem",
                mem_pairs(0, dy),
            )
            low = 0
            for kind, k, _, _ in two:
                place[kind, k, dy] = (f"Y{first + 1}_{dy}", low)
                low += rows_local if kind == "V" else proj_count * columns

    for dc in range(1, nc):
        plan.move(
            f"whole{dc}", "core", 8, ["whole0", "share"], lambda env: env["whole0"], "dp", dp_pairs(0, dc)
        )
    for at in range(nz):
        if at:
            plan.work(
                f"own{at}",
                2,
                ["index", "whole0"] + ([f"X{at - 2}_1_0"] if nx > 1 and at > 1 else ["meta"]),
                lambda env, at=at: pick_blocks(
                    env["index"][at * ny : (at + 1) * ny], env["whole0"], columns, 1
                ),
            )
        for dx in range(1, nx):
            plan.move(
                f"X{at}_{dx}_0",
                "x",
                2,
                [f"own{at}"],
                lambda env, at=at: env[f"own{at}"],
                "dp",
                dp_pairs(dx, 0),
            )
            for dc in range(1, nc):
                plan.move(
                    f"X{at}_{dx}_{dc}",
                    "core",
                    2,
                    [f"X{at}_{dx}_0"],
                    lambda env, at=at, dx=dx: env[f"X{at}_{dx}_0"],
                    "dp",
                    dp_pairs(0, dc),
                )
    wholes = [f"whole{dc}" for dc in range(nc)]
    pieces = [[f"X{at}_{dx}_{dc}" for dx in range(1, nx) for dc in range(nc)] for at in range(nz)]

    steps = [[0]] + [[k for k, _, _ in hops[i : i + 2]] for i in range(0, len(hops), 2)]
    for at, ks in enumerate(steps):
        held = {}
        for k in ks:
            for dy in range(ny):
                name, low = place["V", k, dy]
                held.setdefault(name, []).append((low // rows_local, k * ny + dy))
        for blocks in held.values():
            assert [low for low, _ in sorted(blocks)] == list(range(len(blocks)))
        names = list(held)
        places = [[block for _, block in sorted(held[n])] for n in names]
        before = [f"fetch{at - 1}"] if at else []

        def run(env, names=names, places=places, before=before, last=at == len(steps) - 1):
            return fetch(
                env["meta"],
                per_token,
                rows_local,
                [env[n] for n in names],
                places,
                env[before[0]][0] if before else None,
                proj_count,
                last,
            )

        plan.work(f"fetch{at}", 7 * len(ks), ["meta", *names, *before], run)
    fetched = f"fetch{len(steps) - 1}"

    pairs_of = [list(range(i, min(i + 2, nz))) for i in range(0, nz, 2)]

    def add_part(p, y_needs):
        pair = pairs_of[p]
        plan.work(
            f"part{p}",
            6 * len(pair),
            ["index", fetched, *wholes, *[n for at in pair for n in pieces[at]]],
            lambda env: part(
                env["index"],
                env[fetched][1],
                [env[n] for n in wholes],
                [[env[n] for n in pieces[at]] for at in pair],
                pair[0],
                ny,
                columns,
            ),
        )
        for at in pair:
            for dy in range(1, ny):
                plan.move(
                    f"P{at}_{dy}",
                    "y",
                    1,
                    [f"part{p}", *y_needs],
                    lambda env, place=at % 2 * ny + dy: env[f"part{p}"][place],
                    "mem",
                    mem_pairs(0, -dy),
                )
            if p:
                y_needs = [f"P{at}_{dy}" for dy in range(1, ny)]

    add_part(0, [])

    weights = [place["W", k, dy] for k in order for dy in range(ny)]
    plan.work(
        "project",
        18,
        [
            "index",
            "meta",
            fetched,
            *wholes,
            *[n for piece in pieces for n in piece],
            *dict.fromkeys(n for n, _ in weights),
        ],
        lambda env: project(
            env["index"],
            per_token,
            env["meta"],
            env[fetched][0],
            [env[n] for n in wholes],
            [[env[n] for n in piece] for piece in pieces],
            [env[n] for n, _ in weights],
            [low for _, low in weights],
            proj_count,
            columns,
        ),
    )

    sets = [
        (p, dy) for p in range(len(pairs_of)) for dy in range(ny - 1, -1, -1)
    ]
    cut = max(ny - 1, 1)
    row_sum = {}
    for name, some in (("rows0", sets[:cut]), ("rows1", sets[cut:])):
        for at, one in enumerate(some):
            row_sum[one] = (name, at)
        if some:
            plan.work(
                name,
                5 * len(some),
                ["meta", "project"],
                lambda env, some=some: scatter(
                    [[order[at] * ny + dy for at in pairs_of[p]] for p, dy in some],
                    rows_local,
                    env["meta"],
                    env["project"][0],
                ),
            )
    for p, dy in sets:
        name, at = row_sum[p, dy]
        if dy:
            plan.move(
                f"R{p}_{dy}",
                "y",
                len(pairs_of[p]),
                [name],
                lambda env, name=name, at=at: env[name][at],
                "mem",
                mem_pairs(0, -dy),
            )
    for p in range(1, len(pairs_of)):
        add_part(p, [])

    def y_sum_p(env, at):
        line = env[f"part{at // 2}"][at % 2 * ny].astype(F32)
        for dy in range(1, ny):
            line = line + env[f"P{at}_{dy}"].astype(F32)
        return line

    def y_sum_r(env, at):
        span = slice((at % 2) * rows_local, (at % 2 + 1) * rows_local)
        name, place_ = row_sum[at // 2, 0]
        line = env[name][place_][span].astype(F32)
        for dy in range(1, ny):
            line = line + env[f"R{at // 2}_{dy}"][span].astype(F32)
        return line

    def source_p(at):
        return [f"part{at // 2}"] + [f"P{at}_{dy}" for dy in range(1, ny)]

    def source_r(at):
        return [row_sum[at // 2, 0][0]] + [f"R{at // 2}_{dy}" for dy in range(1, ny)]

    arrivals = {}
    for kind, y_sum, source in (
        ("R", y_sum_r, source_r),
        ("P", y_sum_p, source_p),
    ):
        passed = []
        for k in chain:
            at = order.index(k)

            def operand(env, at=at, passed=tuple(passed), y_sum=y_sum):
                line = y_sum(env, at)
                for name in passed:
                    line = line + env[name].astype(F32)
                return line.astype(BF16)

            plan.move(f"Z{kind}{k}", "z", 1, [*source(at), *passed], operand, "mem", mem_pairs(-1, 0))
            passed = [f"Z{kind}{k}"]
        arrivals[kind] = list(passed)
        if nz > 1:
            at = order.index(nz - 1)
            plan.move(
                f"Z{kind}{nz - 1}",
                "z",
                1,
                source(at),
                lambda env, at=at, y_sum=y_sum: y_sum(env, at).astype(BF16),
                "mem",
                mem_pairs(1, 0),
            )
            arrivals[kind].append(f"Z{kind}{nz - 1}")

    part_rows = rows_local // dp_size

    def my_rows(env):
        total = y_sum_r(env, order.index(0))
        for name in arrivals["R"]:
            total = total + env[name].astype(F32)
        return total.astype(BF16)

    last_r = source_r(order.index(0))
    for g in range(1, dp_size):
        to = ((x + g // nc) % nx) * nc + (c + g % nc) % nc
        plan.move(
            f"T{g}",
            "small",
            1,
            [*last_r, *arrivals["R"]],
            lambda env, to=to: lax.dynamic_slice_in_dim(
                my_rows(env),
                to * part_rows,
                part_rows,
                axis=0,
            ),
            "dp",
            dp_pairs(g // nc, g % nc),
        )

    for g in range(1, dp_size):
        plan.move(
            f"S{g}",
            "small",
            1,
            ["project", *[f"R0_{dy}" for dy in range(1, ny)]],
            lambda env, g=g: env["project"][1][g * tokens_dev : (g + 1) * tokens_dev],
            "dp",
            dp_pairs(-(g // nc), -(g % nc)),
        )

    env = plan.run()

    total = y_sum_p(env, order.index(0))
    for name in arrivals["P"]:
        total = total + env[name].astype(F32)
    proj_grads = total.reshape(proj_count, width, columns)

    score_grads = env["project"][1][:tokens_dev]
    for g in range(1, dp_size):
        score_grads = score_grads + env[f"S{g}"]

    mine = my_rows(env)
    value_grads = jnp.zeros((part_rows, value_width), BF16)
    for g in range(dp_size):
        came = ((x - g // nc) % nx) * nc + (c - g % nc) % nc
        piece = env[f"T{g}"] if g else lax.dynamic_slice_in_dim(mine, dp * part_rows, part_rows, axis=0)
        value_grads = lax.dynamic_update_slice_in_dim(value_grads, piece, came * width, axis=1)
    return (score_grads, value_grads, proj_grads)


def solution(mesh):
    return jax.shard_map(
        local,
        mesh=mesh,
        in_specs=(
            P(("mem", "dp"), None),
            P(("mem", "dp"), None),
            P(("mem", "dp"), None),
            P(("mem", "dp"), None),
            P("mem", None),
            P(None, None, "mem"),
        ),
        out_specs=(P(("mem", "dp"), None), P(("mem", "dp"), None), P(None, "dp", "mem")),
        check_vma=False,
    )
```

```python
import functools

import jax
import jax.numpy as jnp
from jax import lax
from jax.experimental import pallas as pl
from jax.experimental.pallas import tpu as pltpu
from jax.sharding import PartitionSpec as P

F32 = jnp.float32
BF16 = jnp.bfloat16
VMEM_LIMIT = 20 * 1024 * 1024
COST_PART = 16


def params(limit=VMEM_LIMIT):
    return pltpu.CompilerParams(vmem_limit_bytes=limit)


def cost(flops, size):
    return pl.CostEstimate(flops=flops // COST_PART, bytes_accessed=size // COST_PART, transcendentals=0)


def whole_block(shape):
    return pl.BlockSpec(shape, lambda *_: (0,) * len(shape))


def copy_kernel(index_ref, in_ref, out_ref):
    out_ref[...] = in_ref[...]


def pick_blocks(index, a, block, axis):
    count = index.shape[0]
    shape = list(a.shape)
    shape[axis] = count * block
    tile = list(a.shape)
    tile[axis] = block

    def at(k):
        return tuple(k if dim == axis else 0 for dim in range(a.ndim))

    return pl.pallas_call(
        copy_kernel,
        grid_spec=pltpu.PrefetchScalarGridSpec(
            num_scalar_prefetch=1,
            grid=(count,),
            in_specs=[pl.BlockSpec(tuple(tile), lambda i, index_ref: at(index_ref[i]))],
            out_specs=pl.BlockSpec(tuple(tile), lambda i, index_ref: at(i)),
        ),
        out_shape=jax.ShapeDtypeStruct(tuple(shape), a.dtype),
        compiler_params=params(),
        name="pick",
    )(index, a)


def share_kernel(place_ref, index_ref, value_ref, weight_ref, *refs):
    blocks, (share_ref, table_ref, turned_ref, grad_ref) = refs[:-4], refs[-4:]
    count, _, depth = weight_ref.shape
    rows = value_ref.shape[0]
    share_ref[:rows] = value_ref[...]
    table_ref[...] = value_ref[...]
    for j in range(count):
        turned = weight_ref[j].T
        share_ref[rows + j * depth : rows + (j + 1) * depth] = turned
        turned_ref[j * depth : (j + 1) * depth] = turned
    for ky, block in enumerate(blocks):
        grad_ref[:, ky * depth : (ky + 1) * depth] = block[...]


def first_share(place, index, values, proj_w, grad_out, width, ny):
    rows = values.shape[0]
    count, _, depth = proj_w.shape
    tokens = grad_out.shape[0]
    shapes = [
        (rows + count * depth, width),
        (rows, width),
        (count * depth, width),
        (tokens, ny * depth),
    ]
    return pl.pallas_call(
        share_kernel,
        grid_spec=pltpu.PrefetchScalarGridSpec(
            num_scalar_prefetch=2,
            grid=(1,),
            in_specs=[
                pl.BlockSpec((rows, width), lambda i, place_ref, index_ref: (0, place_ref[0])),
                pl.BlockSpec(
                    (count, width, depth), lambda i, place_ref, index_ref: (0, place_ref[0], 0)
                ),
            ]
            + [
                pl.BlockSpec(
                    (tokens, depth), lambda i, place_ref, index_ref, ky=ky: (0, index_ref[ky])
                )
                for ky in range(ny)
            ],
            out_specs=[whole_block(shape) for shape in shapes],
        ),
        out_shape=[jax.ShapeDtypeStruct(shape, BF16) for shape in shapes],
        compiler_params=params(3 * VMEM_LIMIT),
        cost_estimate=cost(0, 6 * rows * width),
        name="share",
    )(place, index, values, proj_w, *[grad_out] * ny)


def fetch_kernel(per_token, proj_count, rows, places, has_total, is_last, meta_ref, *refs):
    if has_total:
        before_ref, refs = refs[0], refs[1:]
    tables, chosen_ref = refs[: len(places)], refs[len(places)]
    width = tables[0].shape[1]
    tile = meta_ref.shape[1]
    meta = meta_ref[...].T
    lane = lax.broadcasted_iota(jnp.int32, (tile, rows), 1)
    mixes = [jnp.zeros((tile, width), F32) for _ in range(proj_count)]
    for s in range(per_token):
        ids = meta[:, s : s + 1].astype(jnp.int32)
        total = jnp.zeros((tile, width), F32)
        for table, blocks in zip(tables, places, strict=True):
            for at, block in enumerate(blocks):
                hot = jnp.where(lane == ids - block * rows, 1.0, 0.0).astype(BF16)
                total += jnp.dot(
                    hot, table[at * rows : (at + 1) * rows], preferred_element_type=F32
                )
        if has_total:
            total += before_ref[s].astype(F32)
        chosen_ref[s] = total.astype(BF16)
        if is_last:
            proj = meta[:, per_token + s : per_token + s + 1]
            score = meta[:, 2 * per_token + s : 2 * per_token + s + 1]
            for j in range(proj_count):
                mixes[j] += jnp.where(proj == j, score, 0.0) * total
    if is_last:
        refs[len(places) + 1][...] = jnp.concatenate(mixes, axis=1).astype(BF16).T


def fetch(meta, per_token, rows, tables, places, before, proj_count, is_last):
    tokens = meta.shape[1]
    width = tables[0].shape[1]
    tile = 512
    picked = pl.BlockSpec((per_token, tile, width), lambda i: (0, i, 0))
    args, specs = [meta], [pl.BlockSpec((meta.shape[0], tile), lambda i: (0, i))]
    if before is not None:
        args.append(before)
        specs.append(picked)
    out_specs = [picked]
    out_shape = [jax.ShapeDtypeStruct((per_token, tokens, width), BF16)]
    if is_last:
        out_specs.append(pl.BlockSpec((proj_count * width, tile), lambda i: (0, i)))
        out_shape.append(jax.ShapeDtypeStruct((proj_count * width, tokens), BF16))
    count = sum(len(blocks) for blocks in places)
    return pl.pallas_call(
        functools.partial(
            fetch_kernel, per_token, proj_count, rows, places, before is not None, is_last
        ),
        grid=(tokens // tile,),
        in_specs=specs
        + [whole_block((len(blocks) * rows, width)) for blocks in places],
        out_specs=out_specs,
        out_shape=out_shape,
        compiler_params=params(),
        cost_estimate=cost(2 * tokens * per_token * rows * count * width, 2 * rows * count * width),
        name="fetch",
    )(*args, *tables)


def part_kernel(near, far, count, steps, index_ref, mix_ref, *refs):
    wholes, refs = refs[:near], refs[near:]
    pieces, outs = refs[: far * count], refs[far * count :]
    ny = len(outs) // count
    for at in range(count):
        for ky in range(ny):
            place = at * ny + ky

            @pl.when(pl.program_id(0) // steps == place)
            def _(at=at, place=place):
                grads = [*wholes, *pieces[at * far : (at + 1) * far]]
                grads = jnp.concatenate([grad[...] for grad in grads], axis=0)
                total = jnp.dot(mix_ref[...], grads, preferred_element_type=F32)
                outs[place][...] = total.astype(BF16)


def part(index, mixes, wholes, pieces, first, ny, columns):
    depth, tokens = mixes.shape
    rows = wholes[0].shape[0]
    tile = 256
    steps = columns // tile
    count, far = len(pieces), len(pieces[0])

    def whole(i, index_ref):
        return (0, index_ref[first * ny + i // steps] * steps + i % steps)

    def within(low, size):
        return lambda i, index_ref: (0, jnp.clip(i - low, 0, size - 1))

    specs = [pl.BlockSpec((rows, tile), whole)] * len(wholes)
    for at in range(count):
        specs += [pl.BlockSpec((rows, tile), within(at * ny * steps, ny * steps))] * far
    return pl.pallas_call(
        functools.partial(part_kernel, len(wholes), far, count, steps),
        grid_spec=pltpu.PrefetchScalarGridSpec(
            num_scalar_prefetch=1,
            grid=(count * ny * steps,),
            in_specs=[whole_block((depth, tokens))] + specs,
            out_specs=[
                pl.BlockSpec((depth, tile), within(place * steps, steps))
                for place in range(count * ny)
            ],
        ),
        out_shape=[jax.ShapeDtypeStruct((depth, columns), BF16)] * (count * ny),
        compiler_params=params(),
        cost_estimate=cost(2 * depth * tokens * columns * count * ny, 2 * (depth * tokens + (tokens + depth) * columns * count * ny)),
        name="part",
    )(index, mixes, *wholes, *[a for piece in pieces for a in piece])


def project_kernel(shape, weight_rows, index_ref, meta_ref, chosen_ref, *refs):
    per_token, nz, ny, near, far, proj_count, depth = shape
    wholes, refs = refs[:near], refs[near:]
    pieces, refs = refs[: far * nz], refs[far * nz :]
    weights, refs = refs[: nz * ny], refs[nz * ny :]
    contrib_ref, sums_ref, total, held, held_weights, sems = refs
    tokens, width = wholes[0].shape[0], chosen_ref.shape[2]
    step = pl.program_id(0)

    def copies(at):
        slot = at % 2
        out = []
        for g in range(near):
            for ky in range(ny):
                low = pl.multiple_of(index_ref[at * ny + ky] * depth, depth)
                out.append(
                    pltpu.make_async_copy(
                        wholes[g].at[:, pl.ds(low, depth)],
                        held.at[slot, g, :, pl.ds(ky * depth, depth)],
                        sems.at[slot, g * ny + ky],
                    )
                )
        for g in range(far):
            out.append(
                pltpu.make_async_copy(
                    pieces[at * far + g], held.at[slot, near + g], sems.at[slot, near * ny + g]
                )
            )
        for ky in range(ny):
            low = weight_rows[at * ny + ky]
            out.append(
                pltpu.make_async_copy(
                    weights[at * ny + ky].at[low : low + proj_count * depth],
                    held_weights.at[slot, ky],
                    sems.at[slot, near * ny + far + ky],
                )
            )
        return out

    for at in range(nz):

        @pl.when(step == at)
        def _(at=at):
            slot = at % 2
            if at == 0:
                for copy in copies(0):
                    copy.start()
            for copy in copies(at):
                copy.wait()
            if at + 1 < nz:
                for copy in copies(at + 1):
                    copy.start()
            weight = jnp.concatenate(
                [
                    jnp.concatenate(
                        [
                            held_weights[slot, ky, j * depth : (j + 1) * depth]
                            for j in range(proj_count)
                        ],
                        axis=1,
                    )
                    for ky in range(ny)
                ],
                axis=0,
            )
            for g in range(near + far):
                span = slice(g * tokens, (g + 1) * tokens)
                term = jnp.dot(held[slot, g], weight, preferred_element_type=F32)
                if at == 0:
                    total[span] = term
                elif at < nz - 1:
                    total[span] += term
                else:
                    projected = total[span] + term
                    meta = meta_ref[:, span].T
                    for s in range(per_token):
                        proj = meta[:, per_token + s : per_token + s + 1]
                        score = meta[:, 2 * per_token + s : 2 * per_token + s + 1]
                        picked = jnp.zeros((tokens, width), F32)
                        for j in range(proj_count):
                            picked = jnp.where(
                                proj == j, projected[:, j * width : (j + 1) * width], picked
                            )
                        contrib_ref[s, span] = (score * picked).astype(BF16)
                        sums_ref[span, s : s + 1] = jnp.sum(
                            picked * chosen_ref[s, span].astype(F32), axis=1, keepdims=True
                        )


def project(index, per_token, meta, chosen, wholes, pieces, weights, weight_rows, proj_count, depth):
    _, total, width = chosen.shape
    nz, far, near = len(pieces), len(pieces[0]), len(wholes)
    ny = len(weights) // nz
    tokens = wholes[0].shape[0]
    sums_shape = (total, per_token)
    room = 4 * total * proj_count * width + 4 * (near + far) * tokens * ny * depth
    room += 6 * ny * proj_count * depth * width + 8 * chosen.size + 1024 * total
    room += room // 8
    return pl.pallas_call(
        functools.partial(
            project_kernel, (per_token, nz, ny, near, far, proj_count, depth), weight_rows
        ),
        grid_spec=pltpu.PrefetchScalarGridSpec(
            num_scalar_prefetch=1,
            grid=(nz,),
            in_specs=[whole_block(meta.shape), whole_block(chosen.shape)]
            + [pl.BlockSpec(memory_space=pl.ANY)] * (near + far * nz + len(weights)),
            out_specs=[whole_block(chosen.shape), whole_block(sums_shape)],
            scratch_shapes=[
                pltpu.VMEM((total, proj_count * width), F32),
                pltpu.VMEM((2, near + far, tokens, ny * depth), BF16),
                pltpu.VMEM((2, ny, proj_count * depth, width), BF16),
                pltpu.SemaphoreType.DMA((2, near * ny + far + ny)),
            ],
        ),
        out_shape=[
            jax.ShapeDtypeStruct(chosen.shape, BF16),
            jax.ShapeDtypeStruct(sums_shape, F32),
        ],
        compiler_params=params(max(VMEM_LIMIT, room)),
        cost_estimate=cost(
            2 * total * depth * len(weights) * width * proj_count,
            2 * total * depth * len(weights),
        ),
        name="project",
    )(index, meta, chosen, *wholes, *[a for piece in pieces for a in piece], *weights)


def scatter_kernel(per_token, sets, steps, meta_ref, contrib_ref, *outs):
    tile, width = outs[0].shape
    tokens = meta_ref.shape[1]
    chunk = min(tokens, 2048)
    step = pl.program_id(0)
    base, at = jnp.int32(0), 0
    for blocks in sets:
        for block in blocks:
            base = jnp.where(step // steps == at, block * steps * tile, base)
            at += 1
    row = base + (step % steps) * tile + lax.broadcasted_iota(jnp.int32, (tile, chunk), 0)
    total = jnp.zeros((tile, width), F32)
    for first in range(0, tokens, chunk):
        for s in range(per_token):
            ids = meta_ref[s : s + 1, first : first + chunk].astype(jnp.int32)
            hot = jnp.where(row == ids, 1.0, 0.0).astype(BF16)
            total += jnp.dot(
                hot, contrib_ref[s, first : first + chunk], preferred_element_type=F32
            )
    low = 0
    for blocks, out in zip(sets, outs, strict=True):

        @pl.when((step >= low) & (step < low + len(blocks) * steps))
        def _(out=out):
            out[...] = total.astype(BF16)

        low += len(blocks) * steps


def scatter(sets, rows, meta, contrib):
    per_token, tokens, width = contrib.shape
    tile = 512
    steps = rows // tile
    out_specs, low = [], 0
    for blocks in sets:
        size = len(blocks) * steps
        out_specs.append(
            pl.BlockSpec(
                (tile, width), lambda i, low=low, size=size: (jnp.clip(i - low, 0, size - 1), 0)
            )
        )
        low += size
    return pl.pallas_call(
        functools.partial(scatter_kernel, per_token, sets, steps),
        grid=(low,),
        in_specs=[whole_block(meta.shape), whole_block(contrib.shape)],
        out_specs=out_specs,
        out_shape=[
            jax.ShapeDtypeStruct((len(blocks) * rows, width), BF16) for blocks in sets
        ],
        compiler_params=params(),
        cost_estimate=cost(2 * low * tile * per_token * tokens * width, 2 * per_token * tokens * width),
        name="scatter",
    )(meta, contrib)


def inner_factor(count):
    inner = 1
    while count % (inner * inner * 4) == 0:
        inner *= 2
    return inner


class Plan:
    def __init__(self, room, work_room):
        self.room, self.work_room = room, work_room
        self.jobs, self.env = [], {}

    def move(self, name, kind, size, needs, operand, axis, pairs):
        self.jobs.append((name, kind, size, needs, operand, axis, pairs))

    def work(self, name, size, needs, run):
        self.jobs.append((name, "work", size, needs, run, None, None))

    def value(self, name, a):
        self.env[name] = a

    def run(self):
        held, env = (), self.env
        while self.jobs:
            ready = set(env)
            moves, works = [], []
            room = dict(self.room)
            for job in self.jobs:
                if job[1] != "work" and set(job[3]) <= ready and job[2] <= room[job[1]]:
                    room[job[1]] -= job[2]
                    moves.append(job)
            ready |= {job[0] for job in moves if job[1] == "core"}
            left = self.work_room
            for job in self.jobs:
                if job[1] == "work" and set(job[3]) <= ready and (job[2] <= left or not works):
                    left -= job[2]
                    ready.add(job[0])
                    works.append(job)
            assert moves or works
            names = set(held) | {n for job in (*moves, *works) for n in job[3] if n in env}
            names = sorted(names)
            if held:
                leaves, tree = jax.tree.flatten([env[n] for n in names])
                passed = jax.tree.unflatten(tree, lax.optimization_barrier(tuple(leaves)))
                env.update(zip(names, passed, strict=True))
            came = [lax.ppermute(job[4](env), job[5], job[6]) for job in moves]
            for a, job in zip(came, moves, strict=True):
                env[job[0]] = a
            for job in works:
                env[job[0]] = job[4](env)
            held = [job[0] for job in (*moves, *works)]
            self.jobs = [job for job in self.jobs if job[0] not in env]
        return env


def local(grad_out, scores, row_ids, proj_ids, values, proj_w):
    mem_size, dp_size = lax.axis_size("mem"), lax.axis_size("dp")
    ny = inner_factor(mem_size)
    nz = mem_size // ny
    nc = 2 if dp_size % 2 == 0 else 1
    nx = dp_size // nc
    mem, dp = lax.axis_index("mem"), lax.axis_index("dp")
    z, y, x, c = mem // ny, mem % ny, dp // nc, dp % nc
    tokens_dev, per_token = scores.shape
    rows_local, value_width = values.shape
    proj_count, _, columns = proj_w.shape
    width = value_width // dp_size

    def mem_pairs(dz, dy):
        return [
            (i * ny + j, ((i + dz) % nz) * ny + (j + dy) % ny)
            for i in range(nz)
            for j in range(ny)
        ]

    def dp_pairs(dx, dc):
        return [
            (i * nc + j, ((i + dx) % nx) * nc + (j + dc) % nc)
            for i in range(nx)
            for j in range(nc)
        ]

    plan = Plan({"y": 2, "z": 2, "x": 2, "core": 8, "small": 8}, 24)
    env = plan.env

    chain = list(range(nz - 2, 0, -1))
    order = chain[:1] + list(range(nz - 1, max(nz - 2, 0), -1)) + chain[1:] + [0]
    kz = jnp.repeat(jnp.array(order, jnp.int32), ny)
    ky = jnp.tile(jnp.arange(ny, dtype=jnp.int32), nz)
    index = ((z - kz) % nz) * ny + (y - ky) % ny

    fields = 3 * per_token
    plan.value(
        "meta0",
        jnp.concatenate(
            [
                row_ids.astype(F32).T,
                proj_ids.astype(F32).T,
                scores.T,
                jnp.zeros((-fields % 8, tokens_dev), F32),
            ],
            axis=0,
        ),
    )
    for g in range(1, dp_size):
        plan.move(
            f"meta{g}", "small", 1, ["meta0"], lambda env: env["meta0"], "dp", dp_pairs(g // nc, g % nc)
        )

    def unpack(env):
        meta = jnp.concatenate([env[f"meta{g}"] for g in range(dp_size)], axis=1)
        all_rows = meta[:per_token].astype(jnp.int32)
        owner = all_rows // rows_local
        turn = ((z - owner // ny) % nz) * ny + (y - owner % ny) % ny
        ids = turn * rows_local + all_rows % rows_local
        return jnp.concatenate([ids.astype(F32), meta[per_token:]], axis=0)

    plan.work("meta", 1, [f"meta{g}" for g in range(dp_size)], unpack)

    plan.value("index", index)
    plan.value("whole0", grad_out)
    plan.value("dp", dp[None].astype(jnp.int32))
    plan.value("values", values)
    plan.value("proj_w", proj_w)
    plan.work(
        "first",
        3,
        ["dp", "index", "values", "proj_w", "whole0"],
        lambda env: first_share(
            env["dp"], env["index"], env["values"], env["proj_w"], env["whole0"], width, ny
        ),
    )
    for at, name in enumerate(("share", "V0", "W0", "own0")):
        plan.work(name, 0, ["first"], lambda env, at=at: env["first"][at])

    hops = ([(1, 0, 1)] if nz > 1 else []) + ([(nz - 1, 0, -1)] if nz > 2 else [])
    hops += [(k, k - 1, 1) for k in range(2, nz - 1)]
    queue = [(kind, *hop) for kind in "VW" for hop in hops]
    place = {("V", 0, 0): ("share", 0), ("W", 0, 0): ("share", rows_local)}
    for dy in range(1, ny):
        plan.move(f"Y0_{dy}", "y", 2, ["share"], lambda env: env["share"], "mem", mem_pairs(0, dy))
        place["V", 0, dy] = (f"Y0_{dy}", 0)
        place["W", 0, dy] = (f"Y0_{dy}", rows_local)
    for kind, k, source, dz in queue:
        plan.move(
            f"{kind}{k}",
            "z",
            1,
            [f"{kind}{source}"],
            lambda env, name=f"{kind}{source}": env[name],
            "mem",
            mem_pairs(dz, 0),
        )
        place[kind, k, 0] = (f"{kind}{k}", 0)
    for first in range(0, len(queue), 2):
        two = queue[first : first + 2]
        names = [f"{kind}{k}" for kind, k, _, _ in two]
        if first + 2 >= len(queue):
            for name, (kind, k, _, _) in zip(names, two, strict=True):
                for dy in range(1, ny):
                    plan.move(
                        f"{name}_{dy}",
                        "y",
                        1,
                        [name],
                        lambda env, name=name: env[name],
                        "mem",
                        mem_pairs(0, dy),
                    )
                    place[kind, k, dy] = (f"{name}_{dy}", 0)
            break
        for dy in range(1, ny):
            plan.move(
                f"Y{first + 1}_{dy}",
                "y",
                2,
                names,
                lambda env, names=names: jnp.concatenate([env[n] for n in names], axis=0),
                "mem",
                mem_pairs(0, dy),
            )
            low = 0
            for kind, k, _, _ in two:
                place[kind, k, dy] = (f"Y{first + 1}_{dy}", low)
                low += rows_local if kind == "V" else proj_count * columns

    for dc in range(1, nc):
        plan.move(
            f"whole{dc}", "core", 8, ["whole0", "share"], lambda env: env["whole0"], "dp", dp_pairs(0, dc)
        )
    for at in range(nz):
        if at:
            plan.work(
                f"own{at}",
                2,
                ["index", "whole0"] + ([f"X{at - 2}_1_0"] if nx > 1 and at > 1 else ["meta"]),
                lambda env, at=at: pick_blocks(
                    env["index"][at * ny : (at + 1) * ny], env["whole0"], columns, 1
                ),
            )
        for dx in range(1, nx):
            plan.move(
                f"X{at}_{dx}_0",
                "x",
                2,
                [f"own{at}"],
                lambda env, at=at: env[f"own{at}"],
                "dp",
                dp_pairs(dx, 0),
            )
            for dc in range(1, nc):
                plan.move(
                    f"X{at}_{dx}_{dc}",
                    "core",
                    2,
                    [f"X{at}_{dx}_0"],
                    lambda env, at=at, dx=dx: env[f"X{at}_{dx}_0"],
                    "dp",
                    dp_pairs(0, dc),
                )
    wholes = [f"whole{dc}" for dc in range(nc)]
    pieces = [[f"X{at}_{dx}_{dc}" for dx in range(1, nx) for dc in range(nc)] for at in range(nz)]

    steps = [[0]] + [[k for k, _, _ in hops[i : i + 2]] for i in range(0, len(hops), 2)]
    for at, ks in enumerate(steps):
        held = {}
        for k in ks:
            for dy in range(ny):
                name, low = place["V", k, dy]
                held.setdefault(name, []).append((low // rows_local, k * ny + dy))
        for blocks in held.values():
            assert [low for low, _ in sorted(blocks)] == list(range(len(blocks)))
        names = list(held)
        places = [[block for _, block in sorted(held[n])] for n in names]
        before = [f"fetch{at - 1}"] if at else []

        def run(env, names=names, places=places, before=before, last=at == len(steps) - 1):
            return fetch(
                env["meta"],
                per_token,
                rows_local,
                [env[n] for n in names],
                places,
                env[before[0]][0] if before else None,
                proj_count,
                last,
            )

        plan.work(f"fetch{at}", 7 * len(ks), ["meta", *names, *before], run)
    fetched = f"fetch{len(steps) - 1}"

    pairs_of = [list(range(i, min(i + 2, nz))) for i in range(0, nz, 2)]

    def add_part(p, y_needs):
        pair = pairs_of[p]
        plan.work(
            f"part{p}",
            6 * len(pair),
            ["index", fetched, *wholes, *[n for at in pair for n in pieces[at]]],
            lambda env: part(
                env["index"],
                env[fetched][1],
                [env[n] for n in wholes],
                [[env[n] for n in pieces[at]] for at in pair],
                pair[0],
                ny,
                columns,
            ),
        )
        for at in pair:
            for dy in range(1, ny):
                plan.move(
                    f"P{at}_{dy}",
                    "y",
                    1,
                    [f"part{p}", *y_needs],
                    lambda env, place=at % 2 * ny + dy: env[f"part{p}"][place],
                    "mem",
                    mem_pairs(0, -dy),
                )
            if p:
                y_needs = [f"P{at}_{dy}" for dy in range(1, ny)]

    add_part(0, [])

    weights = [place["W", k, dy] for k in order for dy in range(ny)]
    plan.work(
        "project",
        18,
        [
            "index",
            "meta",
            fetched,
            *wholes,
            *[n for piece in pieces for n in piece],
            *dict.fromkeys(n for n, _ in weights),
        ],
        lambda env: project(
            env["index"],
            per_token,
            env["meta"],
            env[fetched][0],
            [env[n] for n in wholes],
            [[env[n] for n in piece] for piece in pieces],
            [env[n] for n, _ in weights],
            [low for _, low in weights],
            proj_count,
            columns,
        ),
    )

    sets = [
        (p, dy) for p in range(len(pairs_of)) for dy in range(ny - 1, -1, -1)
    ]
    cut = max(ny - 1, 1)
    row_sum = {}
    for name, some in (("rows0", sets[:cut]), ("rows1", sets[cut:])):
        for at, one in enumerate(some):
            row_sum[one] = (name, at)
        if some:
            plan.work(
                name,
                5 * len(some),
                ["meta", "project"],
                lambda env, some=some: scatter(
                    [[order[at] * ny + dy for at in pairs_of[p]] for p, dy in some],
                    rows_local,
                    env["meta"],
                    env["project"][0],
                ),
            )
    for p, dy in sets:
        name, at = row_sum[p, dy]
        if dy:
            plan.move(
                f"R{p}_{dy}",
                "y",
                len(pairs_of[p]),
                [name],
                lambda env, name=name, at=at: env[name][at],
                "mem",
                mem_pairs(0, -dy),
            )
    for p in range(1, len(pairs_of)):
        add_part(p, [])

    def y_sum_p(env, at):
        line = env[f"part{at // 2}"][at % 2 * ny].astype(F32)
        for dy in range(1, ny):
            line = line + env[f"P{at}_{dy}"].astype(F32)
        return line

    def y_sum_r(env, at):
        span = slice((at % 2) * rows_local, (at % 2 + 1) * rows_local)
        name, place_ = row_sum[at // 2, 0]
        line = env[name][place_][span].astype(F32)
        for dy in range(1, ny):
            line = line + env[f"R{at // 2}_{dy}"][span].astype(F32)
        return line

    def source_p(at):
        return [f"part{at // 2}"] + [f"P{at}_{dy}" for dy in range(1, ny)]

    def source_r(at):
        return [row_sum[at // 2, 0][0]] + [f"R{at // 2}_{dy}" for dy in range(1, ny)]

    arrivals = {}
    for kind, y_sum, source in (
        ("R", y_sum_r, source_r),
        ("P", y_sum_p, source_p),
    ):
        passed = []
        for k in chain:
            at = order.index(k)

            def operand(env, at=at, passed=tuple(passed), y_sum=y_sum):
                line = y_sum(env, at)
                for name in passed:
                    line = line + env[name].astype(F32)
                return line.astype(BF16)

            plan.move(f"Z{kind}{k}", "z", 1, [*source(at), *passed], operand, "mem", mem_pairs(-1, 0))
            passed = [f"Z{kind}{k}"]
        arrivals[kind] = list(passed)
        if nz > 1:
            at = order.index(nz - 1)
            plan.move(
                f"Z{kind}{nz - 1}",
                "z",
                1,
                source(at),
                lambda env, at=at, y_sum=y_sum: y_sum(env, at).astype(BF16),
                "mem",
                mem_pairs(1, 0),
            )
            arrivals[kind].append(f"Z{kind}{nz - 1}")

    part_rows = rows_local // dp_size

    def my_rows(env):
        total = y_sum_r(env, order.index(0))
        for name in arrivals["R"]:
            total = total + env[name].astype(F32)
        return total.astype(BF16)

    last_r = source_r(order.index(0))
    for g in range(1, dp_size):
        to = ((x + g // nc) % nx) * nc + (c + g % nc) % nc
        plan.move(
            f"T{g}",
            "small",
            1,
            [*last_r, *arrivals["R"]],
            lambda env, to=to: lax.dynamic_slice_in_dim(
                my_rows(env),
                to * part_rows,
                part_rows,
                axis=0,
            ),
            "dp",
            dp_pairs(g // nc, g % nc),
        )

    for g in range(1, dp_size):
        plan.move(
            f"S{g}",
            "small",
            1,
            ["project", *[f"R0_{dy}" for dy in range(1, ny)]],
            lambda env, g=g: env["project"][1][g * tokens_dev : (g + 1) * tokens_dev],
            "dp",
            dp_pairs(-(g // nc), -(g % nc)),
        )

    env = plan.run()

    total = y_sum_p(env, order.index(0))
    for name in arrivals["P"]:
        total = total + env[name].astype(F32)
    proj_grads = total.reshape(proj_count, width, columns)

    score_grads = env["project"][1][:tokens_dev]
    for g in range(1, dp_size):
        score_grads = score_grads + env[f"S{g}"]

    mine = my_rows(env)
    value_grads = jnp.zeros((part_rows, value_width), BF16)
    for g in range(dp_size):
        came = ((x - g // nc) % nx) * nc + (c - g % nc) % nc
        piece = env[f"T{g}"] if g else lax.dynamic_slice_in_dim(mine, dp * part_rows, part_rows, axis=0)
        value_grads = lax.dynamic_update_slice_in_dim(value_grads, piece, came * width, axis=1)
    return (score_grads, value_grads, proj_grads)


def solution(mesh):
    return jax.shard_map(
        local,
        mesh=mesh,
        in_specs=(
            P(("mem", "dp"), None),
            P(("mem", "dp"), None),
            P(("mem", "dp"), None),
            P(("mem", "dp"), None),
            P("mem", None),
            P(None, None, "mem"),
        ),
        out_specs=(P(("mem", "dp"), None), P(("mem", "dp"), None), P(None, "dp", "mem")),
        check_vma=False,
    )
```

```python
import functools

import jax
import jax.numpy as jnp
from jax import lax
from jax.experimental import pallas as pl
from jax.experimental.pallas import tpu as pltpu
from jax.sharding import PartitionSpec as P

F32 = jnp.float32
BF16 = jnp.bfloat16
VMEM_LIMIT = 20 * 1024 * 1024
COST_PART = 16


def params(limit=VMEM_LIMIT):
    return pltpu.CompilerParams(vmem_limit_bytes=limit)


def cost(flops, size):
    return pl.CostEstimate(flops=flops // COST_PART, bytes_accessed=size // COST_PART, transcendentals=0)


def whole_block(shape):
    return pl.BlockSpec(shape, lambda *_: (0,) * len(shape))


def copy_kernel(index_ref, in_ref, out_ref):
    out_ref[...] = in_ref[...]


def pick_blocks(index, a, block, axis):
    count = index.shape[0]
    shape = list(a.shape)
    shape[axis] = count * block
    tile = list(a.shape)
    tile[axis] = block

    def at(k):
        return tuple(k if dim == axis else 0 for dim in range(a.ndim))

    return pl.pallas_call(
        copy_kernel,
        grid_spec=pltpu.PrefetchScalarGridSpec(
            num_scalar_prefetch=1,
            grid=(count,),
            in_specs=[pl.BlockSpec(tuple(tile), lambda i, index_ref: at(index_ref[i]))],
            out_specs=pl.BlockSpec(tuple(tile), lambda i, index_ref: at(i)),
        ),
        out_shape=jax.ShapeDtypeStruct(tuple(shape), a.dtype),
        compiler_params=params(),
        name="pick",
    )(index, a)


def share_kernel(place_ref, index_ref, value_ref, weight_ref, *refs):
    blocks, (share_ref, grad_ref) = refs[:-2], refs[-2:]
    count, _, depth = weight_ref.shape
    rows = value_ref.shape[0]
    share_ref[:rows] = value_ref[...]
    for j in range(count):
        share_ref[rows + j * depth : rows + (j + 1) * depth] = weight_ref[j].T
    for ky, block in enumerate(blocks):
        grad_ref[:, ky * depth : (ky + 1) * depth] = block[...]


def first_share(place, index, values, proj_w, grad_out, width, ny):
    rows = values.shape[0]
    count, _, depth = proj_w.shape
    tokens = grad_out.shape[0]
    shapes = [(rows + count * depth, width), (tokens, ny * depth)]
    return pl.pallas_call(
        share_kernel,
        grid_spec=pltpu.PrefetchScalarGridSpec(
            num_scalar_prefetch=2,
            grid=(1,),
            in_specs=[
                pl.BlockSpec((rows, width), lambda i, place_ref, index_ref: (0, place_ref[0])),
                pl.BlockSpec(
                    (count, width, depth), lambda i, place_ref, index_ref: (0, place_ref[0], 0)
                ),
            ]
            + [
                pl.BlockSpec(
                    (tokens, depth), lambda i, place_ref, index_ref, ky=ky: (0, index_ref[ky])
                )
                for ky in range(ny)
            ],
            out_specs=[whole_block(shape) for shape in shapes],
        ),
        out_shape=[jax.ShapeDtypeStruct(shape, BF16) for shape in shapes],
        compiler_params=params(3 * VMEM_LIMIT),
        cost_estimate=cost(0, 6 * rows * width),
        name="share",
    )(place, index, values, proj_w, *[grad_out] * ny)


def fetch_kernel(per_token, proj_count, rows, places, has_total, is_last, meta_ref, *refs):
    if has_total:
        before_ref, refs = refs[0], refs[1:]
    tables, chosen_ref = refs[: len(places)], refs[len(places)]
    width = tables[0].shape[1]
    tile = meta_ref.shape[1]
    meta = meta_ref[...].T
    lane = lax.broadcasted_iota(jnp.int32, (tile, rows), 1)
    mixes = [jnp.zeros((tile, width), F32) for _ in range(proj_count)]
    for s in range(per_token):
        ids = meta[:, s : s + 1].astype(jnp.int32)
        total = jnp.zeros((tile, width), F32)
        for table, blocks in zip(tables, places, strict=True):
            for at, block in enumerate(blocks):
                hot = jnp.where(lane == ids - block * rows, 1.0, 0.0).astype(BF16)
                total += jnp.dot(
                    hot, table[at * rows : (at + 1) * rows], preferred_element_type=F32
                )
        if has_total:
            total += before_ref[s].astype(F32)
        chosen_ref[s] = total.astype(BF16)
        if is_last:
            proj = meta[:, per_token + s : per_token + s + 1]
            score = meta[:, 2 * per_token + s : 2 * per_token + s + 1]
            for j in range(proj_count):
                mixes[j] += jnp.where(proj == j, score, 0.0) * total
    if is_last:
        refs[len(places) + 1][...] = jnp.concatenate(mixes, axis=1).astype(BF16).T


def fetch(meta, per_token, rows, tables, places, before, proj_count, is_last):
    tokens = meta.shape[1]
    width = tables[0].shape[1]
    tile = 512
    picked = pl.BlockSpec((per_token, tile, width), lambda i: (0, i, 0))
    args, specs = [meta], [pl.BlockSpec((meta.shape[0], tile), lambda i: (0, i))]
    if before is not None:
        args.append(before)
        specs.append(picked)
    out_specs = [picked]
    out_shape = [jax.ShapeDtypeStruct((per_token, tokens, width), BF16)]
    if is_last:
        out_specs.append(pl.BlockSpec((proj_count * width, tile), lambda i: (0, i)))
        out_shape.append(jax.ShapeDtypeStruct((proj_count * width, tokens), BF16))
    count = sum(len(blocks) for blocks in places)
    return pl.pallas_call(
        functools.partial(
            fetch_kernel, per_token, proj_count, rows, places, before is not None, is_last
        ),
        grid=(tokens // tile,),
        in_specs=specs
        + [whole_block((len(blocks) * rows, width)) for blocks in places],
        out_specs=out_specs,
        out_shape=out_shape,
        compiler_params=params(),
        cost_estimate=cost(2 * tokens * per_token * rows * count * width, 2 * rows * count * width),
        name="fetch",
    )(*args, *tables)


def part_kernel(near, far, count, steps, index_ref, mix_ref, *refs):
    wholes, refs = refs[:near], refs[near:]
    pieces, outs = refs[: far * count], refs[far * count :]
    ny = len(outs) // count
    for at in range(count):
        for ky in range(ny):
            place = at * ny + ky

            @pl.when(pl.program_id(0) // steps == place)
            def _(at=at, place=place):
                grads = [*wholes, *pieces[at * far : (at + 1) * far]]
                grads = jnp.concatenate([grad[...] for grad in grads], axis=0)
                total = jnp.dot(mix_ref[...], grads, preferred_element_type=F32)
                outs[place][...] = total.astype(BF16)


def part(index, mixes, wholes, pieces, first, ny, columns):
    depth, tokens = mixes.shape
    rows = wholes[0].shape[0]
    tile = 256
    steps = columns // tile
    count, far = len(pieces), len(pieces[0])

    def whole(i, index_ref):
        return (0, index_ref[first * ny + i // steps] * steps + i % steps)

    def within(low, size):
        return lambda i, index_ref: (0, jnp.clip(i - low, 0, size - 1))

    specs = [pl.BlockSpec((rows, tile), whole)] * len(wholes)
    for at in range(count):
        specs += [pl.BlockSpec((rows, tile), within(at * ny * steps, ny * steps))] * far
    return pl.pallas_call(
        functools.partial(part_kernel, len(wholes), far, count, steps),
        grid_spec=pltpu.PrefetchScalarGridSpec(
            num_scalar_prefetch=1,
            grid=(count * ny * steps,),
            in_specs=[whole_block((depth, tokens))] + specs,
            out_specs=[
                pl.BlockSpec((depth, tile), within(place * steps, steps))
                for place in range(count * ny)
            ],
        ),
        out_shape=[jax.ShapeDtypeStruct((depth, columns), BF16)] * (count * ny),
        compiler_params=params(),
        cost_estimate=cost(2 * depth * tokens * columns * count * ny, 2 * (depth * tokens + (tokens + depth) * columns * count * ny)),
        name="part",
    )(index, mixes, *wholes, *[a for piece in pieces for a in piece])


def project_kernel(shape, weight_rows, index_ref, meta_ref, chosen_ref, *refs):
    per_token, nz, ny, near, far, proj_count, depth = shape
    wholes, refs = refs[:near], refs[near:]
    pieces, refs = refs[: far * nz], refs[far * nz :]
    weights, refs = refs[: nz * ny], refs[nz * ny :]
    contrib_ref, sums_ref, total, held, held_weights, sems = refs
    tokens, width = wholes[0].shape[0], chosen_ref.shape[2]
    step = pl.program_id(0)

    def copies(at):
        slot = at % 2
        out = []
        for g in range(near):
            for ky in range(ny):
                low = pl.multiple_of(index_ref[at * ny + ky] * depth, depth)
                out.append(
                    pltpu.make_async_copy(
                        wholes[g].at[:, pl.ds(low, depth)],
                        held.at[slot, g, :, pl.ds(ky * depth, depth)],
                        sems.at[slot, g * ny + ky],
                    )
                )
        for g in range(far):
            out.append(
                pltpu.make_async_copy(
                    pieces[at * far + g], held.at[slot, near + g], sems.at[slot, near * ny + g]
                )
            )
        for ky in range(ny):
            low = weight_rows[at * ny + ky]
            out.append(
                pltpu.make_async_copy(
                    weights[at * ny + ky].at[low : low + proj_count * depth],
                    held_weights.at[slot, ky],
                    sems.at[slot, near * ny + far + ky],
                )
            )
        return out

    for at in range(nz):

        @pl.when(step == at)
        def _(at=at):
            slot = at % 2
            if at == 0:
                for copy in copies(0):
                    copy.start()
            for copy in copies(at):
                copy.wait()
            if at + 1 < nz:
                for copy in copies(at + 1):
                    copy.start()
            weight = jnp.concatenate(
                [
                    jnp.concatenate(
                        [
                            held_weights[slot, ky, j * depth : (j + 1) * depth]
                            for j in range(proj_count)
                        ],
                        axis=1,
                    )
                    for ky in range(ny)
                ],
                axis=0,
            )
            for g in range(near + far):
                span = slice(g * tokens, (g + 1) * tokens)
                term = jnp.dot(held[slot, g], weight, preferred_element_type=F32)
                if at == 0:
                    total[span] = term
                elif at < nz - 1:
                    total[span] += term
                else:
                    projected = total[span] + term
                    meta = meta_ref[:, span].T
                    for s in range(per_token):
                        proj = meta[:, per_token + s : per_token + s + 1]
                        score = meta[:, 2 * per_token + s : 2 * per_token + s + 1]
                        picked = jnp.zeros((tokens, width), F32)
                        for j in range(proj_count):
                            picked = jnp.where(
                                proj == j, projected[:, j * width : (j + 1) * width], picked
                            )
                        contrib_ref[s, span] = (score * picked).astype(BF16)
                        sums_ref[span, s : s + 1] = jnp.sum(
                            picked * chosen_ref[s, span].astype(F32), axis=1, keepdims=True
                        )


def project(index, per_token, meta, chosen, wholes, pieces, weights, weight_rows, proj_count, depth):
    _, total, width = chosen.shape
    nz, far, near = len(pieces), len(pieces[0]), len(wholes)
    ny = len(weights) // nz
    tokens = wholes[0].shape[0]
    sums_shape = (total, per_token)
    room = 4 * total * proj_count * width + 4 * (near + far) * tokens * ny * depth
    room += 6 * ny * proj_count * depth * width + 8 * chosen.size + 1024 * total
    room += room // 8
    return pl.pallas_call(
        functools.partial(
            project_kernel, (per_token, nz, ny, near, far, proj_count, depth), weight_rows
        ),
        grid_spec=pltpu.PrefetchScalarGridSpec(
            num_scalar_prefetch=1,
            grid=(nz,),
            in_specs=[whole_block(meta.shape), whole_block(chosen.shape)]
            + [pl.BlockSpec(memory_space=pl.ANY)] * (near + far * nz + len(weights)),
            out_specs=[whole_block(chosen.shape), whole_block(sums_shape)],
            scratch_shapes=[
                pltpu.VMEM((total, proj_count * width), F32),
                pltpu.VMEM((2, near + far, tokens, ny * depth), BF16),
                pltpu.VMEM((2, ny, proj_count * depth, width), BF16),
                pltpu.SemaphoreType.DMA((2, near * ny + far + ny)),
            ],
        ),
        out_shape=[
            jax.ShapeDtypeStruct(chosen.shape, BF16),
            jax.ShapeDtypeStruct(sums_shape, F32),
        ],
        compiler_params=params(max(VMEM_LIMIT, room)),
        cost_estimate=cost(
            2 * total * depth * len(weights) * width * proj_count,
            2 * total * depth * len(weights),
        ),
        name="project",
    )(index, meta, chosen, *wholes, *[a for piece in pieces for a in piece], *weights)


def scatter_kernel(per_token, sets, steps, meta_ref, contrib_ref, *outs):
    tile, width = outs[0].shape
    tokens = meta_ref.shape[1]
    chunk = min(tokens, 2048)
    step = pl.program_id(0)
    base, at = jnp.int32(0), 0
    for blocks in sets:
        for block in blocks:
            base = jnp.where(step // steps == at, block * steps * tile, base)
            at += 1
    row = base + (step % steps) * tile + lax.broadcasted_iota(jnp.int32, (tile, chunk), 0)
    total = jnp.zeros((tile, width), F32)
    for first in range(0, tokens, chunk):
        for s in range(per_token):
            ids = meta_ref[s : s + 1, first : first + chunk].astype(jnp.int32)
            hot = jnp.where(row == ids, 1.0, 0.0).astype(BF16)
            total += jnp.dot(
                hot, contrib_ref[s, first : first + chunk], preferred_element_type=F32
            )
    low = 0
    for blocks, out in zip(sets, outs, strict=True):

        @pl.when((step >= low) & (step < low + len(blocks) * steps))
        def _(out=out):
            out[...] = total.astype(BF16)

        low += len(blocks) * steps


def scatter(sets, rows, meta, contrib):
    per_token, tokens, width = contrib.shape
    tile = 512
    steps = rows // tile
    out_specs, low = [], 0
    for blocks in sets:
        size = len(blocks) * steps
        out_specs.append(
            pl.BlockSpec(
                (tile, width), lambda i, low=low, size=size: (jnp.clip(i - low, 0, size - 1), 0)
            )
        )
        low += size
    return pl.pallas_call(
        functools.partial(scatter_kernel, per_token, sets, steps),
        grid=(low,),
        in_specs=[whole_block(meta.shape), whole_block(contrib.shape)],
        out_specs=out_specs,
        out_shape=[
            jax.ShapeDtypeStruct((len(blocks) * rows, width), BF16) for blocks in sets
        ],
        compiler_params=params(),
        cost_estimate=cost(2 * low * tile * per_token * tokens * width, 2 * per_token * tokens * width),
        name="scatter",
    )(meta, contrib)


def inner_factor(count):
    inner = 1
    while count % (inner * inner * 4) == 0:
        inner *= 2
    return inner


class Plan:
    def __init__(self, room, work_room):
        self.room, self.work_room = room, work_room
        self.jobs, self.env = [], {}

    def move(self, name, kind, size, needs, operand, axis, pairs):
        self.jobs.append((name, kind, size, needs, operand, axis, pairs))

    def work(self, name, size, needs, run):
        self.jobs.append((name, "work", size, needs, run, None, None))

    def value(self, name, a):
        self.env[name] = a

    def run(self):
        held, env = (), self.env
        while self.jobs:
            ready = set(env)
            moves, works = [], []
            room = dict(self.room)
            for job in self.jobs:
                if job[1] != "work" and set(job[3]) <= ready and job[2] <= room[job[1]]:
                    room[job[1]] -= job[2]
                    moves.append(job)
            ready |= {job[0] for job in moves if job[1] == "core"}
            left = self.work_room
            for job in self.jobs:
                if job[1] == "work" and set(job[3]) <= ready and (job[2] <= left or not works):
                    left -= job[2]
                    ready.add(job[0])
                    works.append(job)
            assert moves or works
            names = set(held) | {n for job in (*moves, *works) for n in job[3] if n in env}
            names = sorted(names)
            if held:
                leaves, tree = jax.tree.flatten([env[n] for n in names])
                passed = jax.tree.unflatten(tree, lax.optimization_barrier(tuple(leaves)))
                env.update(zip(names, passed, strict=True))
            came = [lax.ppermute(job[4](env), job[5], job[6]) for job in moves]
            for a, job in zip(came, moves, strict=True):
                env[job[0]] = a
            for job in works:
                env[job[0]] = job[4](env)
            held = [job[0] for job in (*moves, *works)]
            self.jobs = [job for job in self.jobs if job[0] not in env]
        return env


def local(grad_out, scores, row_ids, proj_ids, values, proj_w):
    mem_size, dp_size = lax.axis_size("mem"), lax.axis_size("dp")
    ny = inner_factor(mem_size)
    nz = mem_size // ny
    nc = 2 if dp_size % 2 == 0 else 1
    nx = dp_size // nc
    mem, dp = lax.axis_index("mem"), lax.axis_index("dp")
    z, y, x, c = mem // ny, mem % ny, dp // nc, dp % nc
    tokens_dev, per_token = scores.shape
    rows_local, value_width = values.shape
    proj_count, _, columns = proj_w.shape
    width = value_width // dp_size

    def mem_pairs(dz, dy):
        return [
            (i * ny + j, ((i + dz) % nz) * ny + (j + dy) % ny)
            for i in range(nz)
            for j in range(ny)
        ]

    def dp_pairs(dx, dc):
        return [
            (i * nc + j, ((i + dx) % nx) * nc + (j + dc) % nc)
            for i in range(nx)
            for j in range(nc)
        ]

    plan = Plan({"y": 2, "z": 2, "x": 2, "core": 9, "small": 8}, 26)
    env = plan.env

    chain = list(range(nz - 2, 0, -1))
    order = chain[:1] + list(range(nz - 1, max(nz - 2, 0), -1)) + chain[1:] + [0]
    kz = jnp.repeat(jnp.array(order, jnp.int32), ny)
    ky = jnp.tile(jnp.arange(ny, dtype=jnp.int32), nz)
    index = ((z - kz) % nz) * ny + (y - ky) % ny

    fields = 3 * per_token
    plan.value(
        "meta0",
        jnp.concatenate(
            [
                row_ids.astype(F32).T,
                proj_ids.astype(F32).T,
                scores.T,
                jnp.zeros((-fields % 8, tokens_dev), F32),
            ],
            axis=0,
        ),
    )
    for g in range(1, dp_size):
        dx, dc = g // nc, g % nc
        if dx and dc:
            before, kind, pairs = f"meta{g - dc}", "core", dp_pairs(0, dc)
        else:
            before, kind, pairs = "meta0", "small", dp_pairs(dx, dc)
        plan.move(f"meta{g}", kind, 1, [before], lambda env, n=before: env[n], "dp", pairs)

    def unpack(env):
        meta = jnp.concatenate([env[f"meta{g}"] for g in range(dp_size)], axis=1)
        all_rows = meta[:per_token].astype(jnp.int32)
        owner = all_rows // rows_local
        turn = ((z - owner // ny) % nz) * ny + (y - owner % ny) % ny
        ids = turn * rows_local + all_rows % rows_local
        return jnp.concatenate([ids.astype(F32), meta[per_token:]], axis=0)

    plan.work("meta", 1, [f"meta{g}" for g in range(dp_size)], unpack)

    plan.value("index", index)
    plan.value("whole0", grad_out)
    plan.value("dp", dp[None].astype(jnp.int32))
    plan.value("values", values)
    plan.value("proj_w", proj_w)
    plan.work(
        "first",
        3,
        ["dp", "index", "values", "proj_w", "whole0"],
        lambda env: first_share(
            env["dp"], env["index"], env["values"], env["proj_w"], env["whole0"], width, ny
        ),
    )
    for at, name in enumerate(("share", "own0")):
        plan.work(name, 0, ["first"], lambda env, at=at: env["first"][at])
    plan.work("V0", 0, ["share", "meta"], lambda env: env["share"][:rows_local])
    plan.work("W0", 0, ["share", "meta"], lambda env: env["share"][rows_local:])

    hops = ([(nz - 1, 0, -1)] if nz > 2 else []) + [(k, k - 1, 1) for k in range(2, nz - 1)]
    queue = [(kind, *hop) for kind in "VW" for hop in hops]
    place = {("V", 0, 0): ("share", 0), ("W", 0, 0): ("share", rows_local)}
    if nz > 1:
        plan.move("next", "z", 2, ["share"], lambda env: env["share"], "mem", mem_pairs(1, 0))
        place["V", 1, 0], place["W", 1, 0] = ("next", 0), ("next", rows_local)
    for k, name in enumerate(["share", "next"][:nz]):
        for dy in range(1, ny):
            plan.move(
                f"Y{name}_{dy}", "y", 2, [name], lambda env, name=name: env[name], "mem", mem_pairs(0, dy)
            )
            place["V", k, dy] = (f"Y{name}_{dy}", 0)
            place["W", k, dy] = (f"Y{name}_{dy}", rows_local)
    for kind, k, source, dz in queue:
        if source == 1:
            span = slice(rows_local) if kind == "V" else slice(rows_local, None)
            needs, operand = ["next"], lambda env, span=span: env["next"][span]
        else:
            needs, operand = [f"{kind}{source}"], lambda env, name=f"{kind}{source}": env[name]
        plan.move(f"{kind}{k}", "z", 1, needs, operand, "mem", mem_pairs(dz, 0))
        place[kind, k, 0] = (f"{kind}{k}", 0)
    for first in range(0, len(queue), 2):
        two = queue[first : first + 2]
        names = [f"{kind}{k}" for kind, k, _, _ in two]
        if first + 2 >= len(queue):
            for name, (kind, k, _, _) in zip(names, two, strict=True):
                for dy in range(1, ny):
                    plan.move(
                        f"{name}_{dy}",
                        "y",
                        1,
                        [name],
                        lambda env, name=name: env[name],
                        "mem",
                        mem_pairs(0, dy),
                    )
                    place[kind, k, dy] = (f"{name}_{dy}", 0)
            break
        for dy in range(1, ny):
            plan.move(
                f"Y{first + 1}_{dy}",
                "y",
                2,
                names,
                lambda env, names=names: jnp.concatenate([env[n] for n in names], axis=0),
                "mem",
                mem_pairs(0, dy),
            )
            low = 0
            for kind, k, _, _ in two:
                place[kind, k, dy] = (f"Y{first + 1}_{dy}", low)
                low += rows_local if kind == "V" else proj_count * columns

    for dc in range(1, nc):
        plan.move(
            f"whole{dc}", "core", 8, ["whole0", "share"], lambda env: env["whole0"], "dp", dp_pairs(0, dc)
        )
    for at in range(nz):
        if at:
            plan.work(
                f"own{at}",
                2,
                ["index", "whole0"] + ([f"X{at - 2}_1_0"] if nx > 1 and at > 1 else ["meta"]),
                lambda env, at=at: pick_blocks(
                    env["index"][at * ny : (at + 1) * ny], env["whole0"], columns, 1
                ),
            )
        for dx in range(1, nx):
            plan.move(
                f"X{at}_{dx}_0",
                "x",
                2,
                [f"own{at}"],
                lambda env, at=at: env[f"own{at}"],
                "dp",
                dp_pairs(dx, 0),
            )
            for dc in range(1, nc):
                plan.move(
                    f"X{at}_{dx}_{dc}",
                    "core",
                    2,
                    [f"X{at}_{dx}_0"],
                    lambda env, at=at, dx=dx: env[f"X{at}_{dx}_0"],
                    "dp",
                    dp_pairs(0, dc),
                )
    wholes = [f"whole{dc}" for dc in range(nc)]
    pieces = [[f"X{at}_{dx}_{dc}" for dx in range(1, nx) for dc in range(nc)] for at in range(nz)]

    steps = [[k] for k in range(min(nz, 2))] + [[k for k, _, _ in hops[i : i + 2]] for i in range(0, len(hops), 2)]
    for at, ks in enumerate(steps):
        held = {}
        for k in ks:
            for dy in range(ny):
                name, low = place["V", k, dy]
                held.setdefault(name, []).append((low // rows_local, k * ny + dy))
        for blocks in held.values():
            assert [low for low, _ in sorted(blocks)] == list(range(len(blocks)))
        names = list(held)
        places = [[block for _, block in sorted(held[n])] for n in names]
        before = [f"fetch{at - 1}"] if at else []

        def run(env, names=names, places=places, before=before, last=at == len(steps) - 1):
            return fetch(
                env["meta"],
                per_token,
                rows_local,
                [env[n] for n in names],
                places,
                env[before[0]][0] if before else None,
                proj_count,
                last,
            )

        plan.work(f"fetch{at}", 7 * len(ks), ["meta", *names, *before], run)
    fetched = f"fetch{len(steps) - 1}"

    pairs_of = [list(range(i, min(i + 2, nz))) for i in range(0, nz, 2)]

    def add_part(p, y_needs):
        pair = pairs_of[p]
        plan.work(
            f"part{p}",
            6 * len(pair),
            ["index", fetched, *wholes, *[n for at in pair for n in pieces[at]]],
            lambda env: part(
                env["index"],
                env[fetched][1],
                [env[n] for n in wholes],
                [[env[n] for n in pieces[at]] for at in pair],
                pair[0],
                ny,
                columns,
            ),
        )
        for at in pair:
            for dy in range(1, ny):
                plan.move(
                    f"P{at}_{dy}",
                    "y",
                    1,
                    [f"part{p}", *y_needs],
                    lambda env, place=at % 2 * ny + dy: env[f"part{p}"][place],
                    "mem",
                    mem_pairs(0, -dy),
                )
            if p:
                y_needs = [f"P{at}_{dy}" for dy in range(1, ny)]

    add_part(0, [])

    weights = [place["W", k, dy] for k in order for dy in range(ny)]
    plan.work(
        "project",
        18,
        [
            "index",
            "meta",
            fetched,
            *wholes,
            *[n for piece in pieces for n in piece],
            *dict.fromkeys(n for n, _ in weights),
        ],
        lambda env: project(
            env["index"],
            per_token,
            env["meta"],
            env[fetched][0],
            [env[n] for n in wholes],
            [[env[n] for n in piece] for piece in pieces],
            [env[n] for n, _ in weights],
            [low for _, low in weights],
            proj_count,
            columns,
        ),
    )

    sets = [
        (p, dy) for p in range(len(pairs_of)) for dy in range(ny - 1, -1, -1)
    ]
    cut = max(ny - 1, 1)
    row_sum = {}
    for name, some in (("rows0", sets[:cut]), ("rows1", sets[cut:])):
        for at, one in enumerate(some):
            row_sum[one] = (name, at)
        if some:
            plan.work(
                name,
                5 * len(some),
                ["meta", "project"],
                lambda env, some=some: scatter(
                    [[order[at] * ny + dy for at in pairs_of[p]] for p, dy in some],
                    rows_local,
                    env["meta"],
                    env["project"][0],
                ),
            )
    for p, dy in sets:
        name, at = row_sum[p, dy]
        if dy:
            plan.move(
                f"R{p}_{dy}",
                "y",
                len(pairs_of[p]),
                [name],
                lambda env, name=name, at=at: env[name][at],
                "mem",
                mem_pairs(0, -dy),
            )
    for p in range(1, len(pairs_of)):
        add_part(p, [])

    def y_sum_p(env, at):
        line = env[f"part{at // 2}"][at % 2 * ny].astype(F32)
        for dy in range(1, ny):
            line = line + env[f"P{at}_{dy}"].astype(F32)
        return line

    def y_sum_r(env, at):
        span = slice((at % 2) * rows_local, (at % 2 + 1) * rows_local)
        name, place_ = row_sum[at // 2, 0]
        line = env[name][place_][span].astype(F32)
        for dy in range(1, ny):
            line = line + env[f"R{at // 2}_{dy}"][span].astype(F32)
        return line

    def source_p(at):
        return [f"part{at // 2}"] + [f"P{at}_{dy}" for dy in range(1, ny)]

    def source_r(at):
        return [row_sum[at // 2, 0][0]] + [f"R{at // 2}_{dy}" for dy in range(1, ny)]

    arrivals = {}
    for kind, y_sum, source in (
        ("R", y_sum_r, source_r),
        ("P", y_sum_p, source_p),
    ):
        passed = []
        for k in chain:
            at = order.index(k)

            def operand(env, at=at, passed=tuple(passed), y_sum=y_sum):
                line = y_sum(env, at)
                for name in passed:
                    line = line + env[name].astype(F32)
                return line.astype(BF16)

            plan.move(f"Z{kind}{k}", "z", 1, [*source(at), *passed], operand, "mem", mem_pairs(-1, 0))
            passed = [f"Z{kind}{k}"]
        arrivals[kind] = list(passed)
        if nz > 1:
            at = order.index(nz - 1)
            plan.move(
                f"Z{kind}{nz - 1}",
                "z",
                1,
                source(at),
                lambda env, at=at, y_sum=y_sum: y_sum(env, at).astype(BF16),
                "mem",
                mem_pairs(1, 0),
            )
            arrivals[kind].append(f"Z{kind}{nz - 1}")

    part_rows = rows_local // dp_size

    def my_rows(env):
        total = y_sum_r(env, order.index(0))
        for name in arrivals["R"]:
            total = total + env[name].astype(F32)
        return total.astype(BF16)

    last_r = source_r(order.index(0))
    for g in range(1, dp_size):
        to = ((x + g // nc) % nx) * nc + (c + g % nc) % nc
        plan.move(
            f"T{g}",
            "small",
            1,
            [*last_r, *arrivals["R"]],
            lambda env, to=to: lax.dynamic_slice_in_dim(
                my_rows(env),
                to * part_rows,
                part_rows,
                axis=0,
            ),
            "dp",
            dp_pairs(g // nc, g % nc),
        )

    for g in range(1, dp_size):
        plan.move(
            f"S{g}",
            "small",
            1,
            ["project", *[f"R0_{dy}" for dy in range(1, ny)]],
            lambda env, g=g: env["project"][1][g * tokens_dev : (g + 1) * tokens_dev],
            "dp",
            dp_pairs(-(g // nc), -(g % nc)),
        )

    env = plan.run()

    total = y_sum_p(env, order.index(0))
    for name in arrivals["P"]:
        total = total + env[name].astype(F32)
    proj_grads = total.reshape(proj_count, width, columns)

    score_grads = env["project"][1][:tokens_dev]
    for g in range(1, dp_size):
        score_grads = score_grads + env[f"S{g}"]

    mine = my_rows(env)
    value_grads = jnp.zeros((part_rows, value_width), BF16)
    for g in range(dp_size):
        came = ((x - g // nc) % nx) * nc + (c - g % nc) % nc
        piece = env[f"T{g}"] if g else lax.dynamic_slice_in_dim(mine, dp * part_rows, part_rows, axis=0)
        value_grads = lax.dynamic_update_slice_in_dim(value_grads, piece, came * width, axis=1)
    return (score_grads, value_grads, proj_grads)


def solution(mesh):
    return jax.shard_map(
        local,
        mesh=mesh,
        in_specs=(
            P(("mem", "dp"), None),
            P(("mem", "dp"), None),
            P(("mem", "dp"), None),
            P(("mem", "dp"), None),
            P("mem", None),
            P(None, None, "mem"),
        ),
        out_specs=(P(("mem", "dp"), None), P(("mem", "dp"), None), P(None, "dp", "mem")),
        check_vma=False,
    )
```

```python
import functools

import jax
import jax.numpy as jnp
from jax import lax
from jax.experimental import pallas as pl
from jax.experimental.pallas import tpu as pltpu
from jax.sharding import PartitionSpec as P

F32 = jnp.float32
BF16 = jnp.bfloat16
VMEM_LIMIT = 20 * 1024 * 1024
COST_PART = 16


def params(limit=VMEM_LIMIT):
    return pltpu.CompilerParams(vmem_limit_bytes=limit)


def cost(flops, size):
    return pl.CostEstimate(flops=flops // COST_PART, bytes_accessed=size // COST_PART, transcendentals=0)


def whole_block(shape):
    return pl.BlockSpec(shape, lambda *_: (0,) * len(shape))


def copy_kernel(index_ref, in_ref, out_ref):
    out_ref[...] = in_ref[...]


def pick_blocks(index, a, block, axis):
    count = index.shape[0]
    shape = list(a.shape)
    shape[axis] = count * block
    tile = list(a.shape)
    tile[axis] = block

    def at(k):
        return tuple(k if dim == axis else 0 for dim in range(a.ndim))

    return pl.pallas_call(
        copy_kernel,
        grid_spec=pltpu.PrefetchScalarGridSpec(
            num_scalar_prefetch=1,
            grid=(count,),
            in_specs=[pl.BlockSpec(tuple(tile), lambda i, index_ref: at(index_ref[i]))],
            out_specs=pl.BlockSpec(tuple(tile), lambda i, index_ref: at(i)),
        ),
        out_shape=jax.ShapeDtypeStruct(tuple(shape), a.dtype),
        compiler_params=params(),
        name="pick",
    )(index, a)


def share_kernel(place_ref, index_ref, value_ref, weight_ref, *refs):
    blocks, (share_ref, grad_ref) = refs[:-2], refs[-2:]
    count, _, depth = weight_ref.shape
    rows = value_ref.shape[0]
    share_ref[:rows] = value_ref[...]
    for j in range(count):
        share_ref[rows + j * depth : rows + (j + 1) * depth] = weight_ref[j].T
    for ky, block in enumerate(blocks):
        grad_ref[:, ky * depth : (ky + 1) * depth] = block[...]


def first_share(place, index, values, proj_w, grad_out, width, ny):
    rows = values.shape[0]
    count, _, depth = proj_w.shape
    tokens = grad_out.shape[0]
    shapes = [(rows + count * depth, width), (tokens, ny * depth)]
    return pl.pallas_call(
        share_kernel,
        grid_spec=pltpu.PrefetchScalarGridSpec(
            num_scalar_prefetch=2,
            grid=(1,),
            in_specs=[
                pl.BlockSpec((rows, width), lambda i, place_ref, index_ref: (0, place_ref[0])),
                pl.BlockSpec(
                    (count, width, depth), lambda i, place_ref, index_ref: (0, place_ref[0], 0)
                ),
            ]
            + [
                pl.BlockSpec(
                    (tokens, depth), lambda i, place_ref, index_ref, ky=ky: (0, index_ref[ky])
                )
                for ky in range(ny)
            ],
            out_specs=[whole_block(shape) for shape in shapes],
        ),
        out_shape=[jax.ShapeDtypeStruct(shape, BF16) for shape in shapes],
        compiler_params=params(3 * VMEM_LIMIT),
        cost_estimate=cost(0, 6 * rows * width),
        name="share",
    )(place, index, values, proj_w, *[grad_out] * ny)


def fetch_kernel(per_token, proj_count, rows, places, has_total, is_last, meta_ref, *refs):
    if has_total:
        before_ref, refs = refs[0], refs[1:]
    tables, chosen_ref = refs[: len(places)], refs[len(places)]
    width = tables[0].shape[1]
    tile = meta_ref.shape[1]
    meta = meta_ref[...].T
    lane = lax.broadcasted_iota(jnp.int32, (tile, rows), 1)
    mixes = [jnp.zeros((tile, width), F32) for _ in range(proj_count)]
    for s in range(per_token):
        ids = meta[:, s : s + 1].astype(jnp.int32)
        total = jnp.zeros((tile, width), F32)
        for table, blocks in zip(tables, places, strict=True):
            for at, block in enumerate(blocks):
                hot = jnp.where(lane == ids - block * rows, 1.0, 0.0).astype(BF16)
                total += jnp.dot(
                    hot, table[at * rows : (at + 1) * rows], preferred_element_type=F32
                )
        if has_total:
            total += before_ref[s].astype(F32)
        chosen_ref[s] = total.astype(BF16)
        if is_last:
            proj = meta[:, per_token + s : per_token + s + 1]
            score = meta[:, 2 * per_token + s : 2 * per_token + s + 1]
            for j in range(proj_count):
                mixes[j] += jnp.where(proj == j, score, 0.0) * total
    if is_last:
        refs[len(places) + 1][...] = jnp.concatenate(mixes, axis=1).astype(BF16).T


def fetch(meta, per_token, rows, tables, places, before, proj_count, is_last):
    tokens = meta.shape[1]
    width = tables[0].shape[1]
    tile = 512
    picked = pl.BlockSpec((per_token, tile, width), lambda i: (0, i, 0))
    args, specs = [meta], [pl.BlockSpec((meta.shape[0], tile), lambda i: (0, i))]
    if before is not None:
        args.append(before)
        specs.append(picked)
    out_specs = [picked]
    out_shape = [jax.ShapeDtypeStruct((per_token, tokens, width), BF16)]
    if is_last:
        out_specs.append(pl.BlockSpec((proj_count * width, tile), lambda i: (0, i)))
        out_shape.append(jax.ShapeDtypeStruct((proj_count * width, tokens), BF16))
    count = sum(len(blocks) for blocks in places)
    return pl.pallas_call(
        functools.partial(
            fetch_kernel, per_token, proj_count, rows, places, before is not None, is_last
        ),
        grid=(tokens // tile,),
        in_specs=specs
        + [whole_block((len(blocks) * rows, width)) for blocks in places],
        out_specs=out_specs,
        out_shape=out_shape,
        compiler_params=params(),
        cost_estimate=cost(2 * tokens * per_token * rows * count * width, 2 * rows * count * width),
        name="fetch",
    )(*args, *tables)


def part_kernel(near, far, count, steps, index_ref, mix_ref, *refs):
    wholes, refs = refs[:near], refs[near:]
    pieces, outs = refs[: far * count], refs[far * count :]
    ny = len(outs) // count
    for at in range(count):
        for ky in range(ny):
            place = at * ny + ky

            @pl.when(pl.program_id(0) // steps == place)
            def _(at=at, place=place):
                grads = [*wholes, *pieces[at * far : (at + 1) * far]]
                grads = jnp.concatenate([grad[...] for grad in grads], axis=0)
                total = jnp.dot(mix_ref[...], grads, preferred_element_type=F32)
                outs[place][...] = total.astype(BF16)


def part(index, mixes, wholes, pieces, first, ny, columns):
    depth, tokens = mixes.shape
    rows = wholes[0].shape[0]
    tile = 256
    steps = columns // tile
    count, far = len(pieces), len(pieces[0])

    def whole(i, index_ref):
        return (0, index_ref[first * ny + i // steps] * steps + i % steps)

    def within(low, size):
        return lambda i, index_ref: (0, jnp.clip(i - low, 0, size - 1))

    specs = [pl.BlockSpec((rows, tile), whole)] * len(wholes)
    for at in range(count):
        specs += [pl.BlockSpec((rows, tile), within(at * ny * steps, ny * steps))] * far
    return pl.pallas_call(
        functools.partial(part_kernel, len(wholes), far, count, steps),
        grid_spec=pltpu.PrefetchScalarGridSpec(
            num_scalar_prefetch=1,
            grid=(count * ny * steps,),
            in_specs=[whole_block((depth, tokens))] + specs,
            out_specs=[
                pl.BlockSpec((depth, tile), within(place * steps, steps))
                for place in range(count * ny)
            ],
        ),
        out_shape=[jax.ShapeDtypeStruct((depth, columns), BF16)] * (count * ny),
        compiler_params=params(),
        cost_estimate=cost(2 * depth * tokens * columns * count * ny, 2 * (depth * tokens + (tokens + depth) * columns * count * ny)),
        name="part",
    )(index, mixes, *wholes, *[a for piece in pieces for a in piece])


def project_kernel(shape, weight_rows, index_ref, meta_ref, chosen_ref, *refs):
    per_token, nz, ny, near, far, proj_count, depth = shape
    wholes, refs = refs[:near], refs[near:]
    pieces, refs = refs[: far * nz], refs[far * nz :]
    weights, refs = refs[: nz * ny], refs[nz * ny :]
    contrib_ref, sums_ref, total, held, held_weights, sems = refs
    tokens, width = wholes[0].shape[0], chosen_ref.shape[2]
    step = pl.program_id(0)

    def copies(at):
        slot = at % 2
        out = []
        for g in range(near):
            for ky in range(ny):
                low = pl.multiple_of(index_ref[at * ny + ky] * depth, depth)
                out.append(
                    pltpu.make_async_copy(
                        wholes[g].at[:, pl.ds(low, depth)],
                        held.at[slot, g, :, pl.ds(ky * depth, depth)],
                        sems.at[slot, g * ny + ky],
                    )
                )
        for g in range(far):
            out.append(
                pltpu.make_async_copy(
                    pieces[at * far + g], held.at[slot, near + g], sems.at[slot, near * ny + g]
                )
            )
        for ky in range(ny):
            low = weight_rows[at * ny + ky]
            out.append(
                pltpu.make_async_copy(
                    weights[at * ny + ky].at[low : low + proj_count * depth],
                    held_weights.at[slot, ky],
                    sems.at[slot, near * ny + far + ky],
                )
            )
        return out

    for at in range(nz):

        @pl.when(step == at)
        def _(at=at):
            slot = at % 2
            if at == 0:
                for copy in copies(0):
                    copy.start()
            for copy in copies(at):
                copy.wait()
            if at + 1 < nz:
                for copy in copies(at + 1):
                    copy.start()
            weight = jnp.concatenate(
                [
                    jnp.concatenate(
                        [
                            held_weights[slot, ky, j * depth : (j + 1) * depth]
                            for j in range(proj_count)
                        ],
                        axis=1,
                    )
                    for ky in range(ny)
                ],
                axis=0,
            )
            for g in range(near + far):
                span = slice(g * tokens, (g + 1) * tokens)
                term = jnp.dot(held[slot, g], weight, preferred_element_type=F32)
                if at == 0:
                    total[span] = term
                elif at < nz - 1:
                    total[span] += term
                else:
                    projected = total[span] + term
                    meta = meta_ref[:, span].T
                    for s in range(per_token):
                        proj = meta[:, per_token + s : per_token + s + 1]
                        score = meta[:, 2 * per_token + s : 2 * per_token + s + 1]
                        picked = jnp.zeros((tokens, width), F32)
                        for j in range(proj_count):
                            picked = jnp.where(
                                proj == j, projected[:, j * width : (j + 1) * width], picked
                            )
                        contrib_ref[s, span] = (score * picked).astype(BF16)
                        sums_ref[span, s : s + 1] = jnp.sum(
                            picked * chosen_ref[s, span].astype(F32), axis=1, keepdims=True
                        )


def project(index, per_token, meta, chosen, wholes, pieces, weights, weight_rows, proj_count, depth):
    _, total, width = chosen.shape
    nz, far, near = len(pieces), len(pieces[0]), len(wholes)
    ny = len(weights) // nz
    tokens = wholes[0].shape[0]
    sums_shape = (total, per_token)
    room = 4 * total * proj_count * width + 4 * (near + far) * tokens * ny * depth
    room += 6 * ny * proj_count * depth * width + 8 * chosen.size + 1024 * total
    room += room // 8
    return pl.pallas_call(
        functools.partial(
            project_kernel, (per_token, nz, ny, near, far, proj_count, depth), weight_rows
        ),
        grid_spec=pltpu.PrefetchScalarGridSpec(
            num_scalar_prefetch=1,
            grid=(nz,),
            in_specs=[whole_block(meta.shape), whole_block(chosen.shape)]
            + [pl.BlockSpec(memory_space=pl.ANY)] * (near + far * nz + len(weights)),
            out_specs=[whole_block(chosen.shape), whole_block(sums_shape)],
            scratch_shapes=[
                pltpu.VMEM((total, proj_count * width), F32),
                pltpu.VMEM((2, near + far, tokens, ny * depth), BF16),
                pltpu.VMEM((2, ny, proj_count * depth, width), BF16),
                pltpu.SemaphoreType.DMA((2, near * ny + far + ny)),
            ],
        ),
        out_shape=[
            jax.ShapeDtypeStruct(chosen.shape, BF16),
            jax.ShapeDtypeStruct(sums_shape, F32),
        ],
        compiler_params=params(max(VMEM_LIMIT, room)),
        cost_estimate=cost(
            2 * total * depth * len(weights) * width * proj_count,
            2 * total * depth * len(weights),
        ),
        name="project",
    )(index, meta, chosen, *wholes, *[a for piece in pieces for a in piece], *weights)


def scatter_kernel(per_token, sets, steps, meta_ref, contrib_ref, *outs):
    tile, width = outs[0].shape
    tokens = meta_ref.shape[1]
    chunk = min(tokens, 2048)
    step = pl.program_id(0)
    base, at = jnp.int32(0), 0
    for blocks in sets:
        for block in blocks:
            base = jnp.where(step // steps == at, block * steps * tile, base)
            at += 1
    row = base + (step % steps) * tile + lax.broadcasted_iota(jnp.int32, (tile, chunk), 0)
    total = jnp.zeros((tile, width), F32)
    for first in range(0, tokens, chunk):
        for s in range(per_token):
            ids = meta_ref[s : s + 1, first : first + chunk].astype(jnp.int32)
            hot = jnp.where(row == ids, 1.0, 0.0).astype(BF16)
            total += jnp.dot(
                hot, contrib_ref[s, first : first + chunk], preferred_element_type=F32
            )
    low = 0
    for blocks, out in zip(sets, outs, strict=True):

        @pl.when((step >= low) & (step < low + len(blocks) * steps))
        def _(out=out):
            out[...] = total.astype(BF16)

        low += len(blocks) * steps


def scatter(sets, rows, meta, contrib):
    per_token, tokens, width = contrib.shape
    tile = 512
    steps = rows // tile
    out_specs, low = [], 0
    for blocks in sets:
        size = len(blocks) * steps
        out_specs.append(
            pl.BlockSpec(
                (tile, width), lambda i, low=low, size=size: (jnp.clip(i - low, 0, size - 1), 0)
            )
        )
        low += size
    return pl.pallas_call(
        functools.partial(scatter_kernel, per_token, sets, steps),
        grid=(low,),
        in_specs=[whole_block(meta.shape), whole_block(contrib.shape)],
        out_specs=out_specs,
        out_shape=[
            jax.ShapeDtypeStruct((len(blocks) * rows, width), BF16) for blocks in sets
        ],
        compiler_params=params(),
        cost_estimate=cost(2 * low * tile * per_token * tokens * width, 2 * per_token * tokens * width),
        name="scatter",
    )(meta, contrib)


def inner_factor(count):
    inner = 1
    while count % (inner * inner * 4) == 0:
        inner *= 2
    return inner


class Plan:
    def __init__(self, room, work_room):
        self.room, self.work_room = room, work_room
        self.jobs, self.env = [], {}

    def move(self, name, kind, size, needs, operand, axis, pairs):
        self.jobs.append((name, kind, size, needs, operand, axis, pairs))

    def work(self, name, size, needs, run):
        self.jobs.append((name, "work", size, needs, run, None, None))

    def value(self, name, a):
        self.env[name] = a

    def run(self):
        held, env = (), self.env
        while self.jobs:
            ready = set(env)
            moves, works = [], []
            room = dict(self.room)
            for job in self.jobs:
                if job[1] != "work" and set(job[3]) <= ready and job[2] <= room[job[1]]:
                    room[job[1]] -= job[2]
                    moves.append(job)
            ready |= {job[0] for job in moves if job[1] == "core"}
            left = self.work_room
            for job in self.jobs:
                if job[1] == "work" and set(job[3]) <= ready and (job[2] <= left or not works):
                    left -= job[2]
                    ready.add(job[0])
                    works.append(job)
            assert moves or works
            names = set(held) | {n for job in (*moves, *works) for n in job[3] if n in env}
            names = sorted(names)
            if held:
                leaves, tree = jax.tree.flatten([env[n] for n in names])
                passed = jax.tree.unflatten(tree, lax.optimization_barrier(tuple(leaves)))
                env.update(zip(names, passed, strict=True))
            came = [lax.ppermute(job[4](env), job[5], job[6]) for job in moves]
            for a, job in zip(came, moves, strict=True):
                env[job[0]] = a
            for job in works:
                env[job[0]] = job[4](env)
            held = [job[0] for job in (*moves, *works)]
            self.jobs = [job for job in self.jobs if job[0] not in env]
        return env


def local(grad_out, scores, row_ids, proj_ids, values, proj_w):
    mem_size, dp_size = lax.axis_size("mem"), lax.axis_size("dp")
    ny = inner_factor(mem_size)
    nz = mem_size // ny
    nc = 2 if dp_size % 2 == 0 else 1
    nx = dp_size // nc
    mem, dp = lax.axis_index("mem"), lax.axis_index("dp")
    z, y, x, c = mem // ny, mem % ny, dp // nc, dp % nc
    tokens_dev, per_token = scores.shape
    rows_local, value_width = values.shape
    proj_count, _, columns = proj_w.shape
    width = value_width // dp_size

    def mem_pairs(dz, dy):
        return [
            (i * ny + j, ((i + dz) % nz) * ny + (j + dy) % ny)
            for i in range(nz)
            for j in range(ny)
        ]

    def dp_pairs(dx, dc):
        return [
            (i * nc + j, ((i + dx) % nx) * nc + (j + dc) % nc)
            for i in range(nx)
            for j in range(nc)
        ]

    plan = Plan({"y": 2, "z": 2, "x": 2, "core": 9, "small": 8}, 26)
    env = plan.env

    chain = list(range(nz - 2, 0, -1))
    order = chain[:1] + list(range(nz - 1, max(nz - 2, 0), -1)) + chain[1:] + [0]
    kz = jnp.repeat(jnp.array(order, jnp.int32), ny)
    ky = jnp.tile(jnp.arange(ny, dtype=jnp.int32), nz)
    index = ((z - kz) % nz) * ny + (y - ky) % ny

    fields = 3 * per_token
    plan.value(
        "meta0",
        jnp.concatenate(
            [
                row_ids.astype(F32).T,
                proj_ids.astype(F32).T,
                scores.T,
                jnp.zeros((-fields % 8, tokens_dev), F32),
            ],
            axis=0,
        ),
    )
    near = [f"meta{dc}" for dc in range(nc)]
    for dc in range(1, nc):
        plan.move(near[dc], "small", 1, ["meta0"], lambda env: env["meta0"], "dp", dp_pairs(0, dc))
    far = [f"metax{dx}" for dx in range(1, nx)]
    for dx in range(1, nx):
        plan.move(
            f"metax{dx}",
            "small",
            1,
            near,
            lambda env: jnp.concatenate([env[n] for n in near], axis=1),
            "dp",
            dp_pairs(dx, 0),
        )

    def unpack(env):
        meta = jnp.concatenate([env[n] for n in (*near, *far)], axis=1)
        all_rows = meta[:per_token].astype(jnp.int32)
        owner = all_rows // rows_local
        turn = ((z - owner // ny) % nz) * ny + (y - owner % ny) % ny
        ids = turn * rows_local + all_rows % rows_local
        return jnp.concatenate([ids.astype(F32), meta[per_token:]], axis=0)

    plan.work("meta", 1, [*near, *far], unpack)

    plan.value("index", index)
    plan.value("whole0", grad_out)
    plan.value("dp", dp[None].astype(jnp.int32))
    plan.value("values", values)
    plan.value("proj_w", proj_w)
    plan.work(
        "first",
        3,
        ["dp", "index", "values", "proj_w", "whole0"],
        lambda env: first_share(
            env["dp"], env["index"], env["values"], env["proj_w"], env["whole0"], width, ny
        ),
    )
    for at, name in enumerate(("share", "own0")):
        plan.work(name, 0, ["first"], lambda env, at=at: env["first"][at])
    plan.work("V0", 0, ["share", near[-1]], lambda env: env["share"][:rows_local])
    plan.work("W0", 0, ["share", near[-1]], lambda env: env["share"][rows_local:])

    hops = ([(nz - 1, 0, -1)] if nz > 2 else []) + [(k, k - 1, 1) for k in range(2, nz - 1)]
    queue = [(kind, *hop) for kind in "VW" for hop in hops]
    place = {("V", 0, 0): ("share", 0), ("W", 0, 0): ("share", rows_local)}
    if nz > 1:
        plan.move("next", "z", 2, ["share"], lambda env: env["share"], "mem", mem_pairs(1, 0))
        place["V", 1, 0], place["W", 1, 0] = ("next", 0), ("next", rows_local)
    for k, name in enumerate(["share", "next"][:nz]):
        for dy in range(1, ny):
            plan.move(
                f"Y{name}_{dy}", "y", 2, [name], lambda env, name=name: env[name], "mem", mem_pairs(0, dy)
            )
            place["V", k, dy] = (f"Y{name}_{dy}", 0)
            place["W", k, dy] = (f"Y{name}_{dy}", rows_local)
    for kind, k, source, dz in queue:
        if source == 1:
            span = slice(rows_local) if kind == "V" else slice(rows_local, None)
            needs, operand = ["next"], lambda env, span=span: env["next"][span]
        else:
            needs, operand = [f"{kind}{source}"], lambda env, name=f"{kind}{source}": env[name]
        plan.move(f"{kind}{k}", "z", 1, needs, operand, "mem", mem_pairs(dz, 0))
        place[kind, k, 0] = (f"{kind}{k}", 0)
    for first in range(0, len(queue), 2):
        two = queue[first : first + 2]
        names = [f"{kind}{k}" for kind, k, _, _ in two]
        if first + 2 >= len(queue):
            for name, (kind, k, _, _) in zip(names, two, strict=True):
                for dy in range(1, ny):
                    plan.move(
                        f"{name}_{dy}",
                        "y",
                        1,
                        [name],
                        lambda env, name=name: env[name],
                        "mem",
                        mem_pairs(0, dy),
                    )
                    place[kind, k, dy] = (f"{name}_{dy}", 0)
            break
        for dy in range(1, ny):
            plan.move(
                f"Y{first + 1}_{dy}",
                "y",
                2,
                names,
                lambda env, names=names: jnp.concatenate([env[n] for n in names], axis=0),
                "mem",
                mem_pairs(0, dy),
            )
            low = 0
            for kind, k, _, _ in two:
                place[kind, k, dy] = (f"Y{first + 1}_{dy}", low)
                low += rows_local if kind == "V" else proj_count * columns

    for dc in range(1, nc):
        plan.move(
            f"whole{dc}", "core", 8, ["whole0", "share"], lambda env: env["whole0"], "dp", dp_pairs(0, dc)
        )
    for at in range(nz):
        if at:
            plan.work(
                f"own{at}",
                2,
                ["index", "whole0"] + ([f"X{at - 2}_1_0"] if nx > 1 and at > 1 else [near[-1]]),
                lambda env, at=at: pick_blocks(
                    env["index"][at * ny : (at + 1) * ny], env["whole0"], columns, 1
                ),
            )
        for dx in range(1, nx):
            plan.move(
                f"X{at}_{dx}_0",
                "x",
                2,
                [f"own{at}"],
                lambda env, at=at: env[f"own{at}"],
                "dp",
                dp_pairs(dx, 0),
            )
            for dc in range(1, nc):
                plan.move(
                    f"X{at}_{dx}_{dc}",
                    "core",
                    2,
                    [f"X{at}_{dx}_0"],
                    lambda env, at=at, dx=dx: env[f"X{at}_{dx}_0"],
                    "dp",
                    dp_pairs(0, dc),
                )
    wholes = [f"whole{dc}" for dc in range(nc)]
    pieces = [[f"X{at}_{dx}_{dc}" for dx in range(1, nx) for dc in range(nc)] for at in range(nz)]

    steps = [[k] for k in range(min(nz, 2))] + [[k for k, _, _ in hops[i : i + 2]] for i in range(0, len(hops), 2)]
    for at, ks in enumerate(steps):
        held = {}
        for k in ks:
            for dy in range(ny):
                name, low = place["V", k, dy]
                held.setdefault(name, []).append((low // rows_local, k * ny + dy))
        for blocks in held.values():
            assert [low for low, _ in sorted(blocks)] == list(range(len(blocks)))
        names = list(held)
        places = [[block for _, block in sorted(held[n])] for n in names]
        before = [f"fetch{at - 1}"] if at else []

        def run(env, names=names, places=places, before=before, last=at == len(steps) - 1):
            return fetch(
                env["meta"],
                per_token,
                rows_local,
                [env[n] for n in names],
                places,
                env[before[0]][0] if before else None,
                proj_count,
                last,
            )

        plan.work(f"fetch{at}", 7 * len(ks), ["meta", *names, *before], run)
    fetched = f"fetch{len(steps) - 1}"

    pairs_of = [list(range(i, min(i + 2, nz))) for i in range(0, nz, 2)]

    def add_part(p, y_needs):
        pair = pairs_of[p]
        plan.work(
            f"part{p}",
            6 * len(pair),
            ["index", fetched, *wholes, *[n for at in pair for n in pieces[at]]],
            lambda env: part(
                env["index"],
                env[fetched][1],
                [env[n] for n in wholes],
                [[env[n] for n in pieces[at]] for at in pair],
                pair[0],
                ny,
                columns,
            ),
        )
        for at in pair:
            for dy in range(1, ny):
                plan.move(
                    f"P{at}_{dy}",
                    "y",
                    1,
                    [f"part{p}", *y_needs],
                    lambda env, place=at % 2 * ny + dy: env[f"part{p}"][place],
                    "mem",
                    mem_pairs(0, -dy),
                )
            if p:
                y_needs = [f"P{at}_{dy}" for dy in range(1, ny)]

    add_part(0, [])

    weights = [place["W", k, dy] for k in order for dy in range(ny)]
    plan.work(
        "project",
        18,
        [
            "index",
            "meta",
            fetched,
            *wholes,
            *[n for piece in pieces for n in piece],
            *dict.fromkeys(n for n, _ in weights),
        ],
        lambda env: project(
            env["index"],
            per_token,
            env["meta"],
            env[fetched][0],
            [env[n] for n in wholes],
            [[env[n] for n in piece] for piece in pieces],
            [env[n] for n, _ in weights],
            [low for _, low in weights],
            proj_count,
            columns,
        ),
    )

    sets = [
        (p, dy) for p in range(len(pairs_of)) for dy in range(ny - 1, -1, -1)
    ]
    cut = max(ny - 1, 1)
    row_sum = {}
    for name, some in (("rows0", sets[:cut]), ("rows1", sets[cut:])):
        for at, one in enumerate(some):
            row_sum[one] = (name, at)
        if some:
            plan.work(
                name,
                5 * len(some),
                ["meta", "project"],
                lambda env, some=some: scatter(
                    [[order[at] * ny + dy for at in pairs_of[p]] for p, dy in some],
                    rows_local,
                    env["meta"],
                    env["project"][0],
                ),
            )
    for p, dy in sets:
        name, at = row_sum[p, dy]
        if dy:
            plan.move(
                f"R{p}_{dy}",
                "y",
                len(pairs_of[p]),
                [name],
                lambda env, name=name, at=at: env[name][at],
                "mem",
                mem_pairs(0, -dy),
            )
    for p in range(1, len(pairs_of)):
        add_part(p, [])

    def y_sum_p(env, at):
        line = env[f"part{at // 2}"][at % 2 * ny].astype(F32)
        for dy in range(1, ny):
            line = line + env[f"P{at}_{dy}"].astype(F32)
        return line

    def y_sum_r(env, at):
        span = slice((at % 2) * rows_local, (at % 2 + 1) * rows_local)
        name, place_ = row_sum[at // 2, 0]
        line = env[name][place_][span].astype(F32)
        for dy in range(1, ny):
            line = line + env[f"R{at // 2}_{dy}"][span].astype(F32)
        return line

    def source_p(at):
        return [f"part{at // 2}"] + [f"P{at}_{dy}" for dy in range(1, ny)]

    def source_r(at):
        return [row_sum[at // 2, 0][0]] + [f"R{at // 2}_{dy}" for dy in range(1, ny)]

    arrivals = {}
    for kind, y_sum, source in (
        ("R", y_sum_r, source_r),
        ("P", y_sum_p, source_p),
    ):
        passed = []
        for k in chain:
            at = order.index(k)

            def operand(env, at=at, passed=tuple(passed), y_sum=y_sum):
                line = y_sum(env, at)
                for name in passed:
                    line = line + env[name].astype(F32)
                return line.astype(BF16)

            plan.move(f"Z{kind}{k}", "z", 1, [*source(at), *passed], operand, "mem", mem_pairs(-1, 0))
            passed = [f"Z{kind}{k}"]
        arrivals[kind] = list(passed)
        if nz > 1:
            at = order.index(nz - 1)
            plan.move(
                f"Z{kind}{nz - 1}",
                "z",
                1,
                source(at),
                lambda env, at=at, y_sum=y_sum: y_sum(env, at).astype(BF16),
                "mem",
                mem_pairs(1, 0),
            )
            arrivals[kind].append(f"Z{kind}{nz - 1}")

    part_rows = rows_local // dp_size

    def my_rows(env):
        total = y_sum_r(env, order.index(0))
        for name in arrivals["R"]:
            total = total + env[name].astype(F32)
        return total.astype(BF16)

    last_r = source_r(order.index(0))
    for g in range(1, dp_size):
        to = ((x + g // nc) % nx) * nc + (c + g % nc) % nc
        plan.move(
            f"T{g}",
            "small",
            1,
            [*last_r, *arrivals["R"]],
            lambda env, to=to: lax.dynamic_slice_in_dim(
                my_rows(env),
                to * part_rows,
                part_rows,
                axis=0,
            ),
            "dp",
            dp_pairs(g // nc, g % nc),
        )

    for g in range(1, dp_size):
        plan.move(
            f"S{g}",
            "small",
            1,
            ["project", *[f"R0_{dy}" for dy in range(1, ny)]],
            lambda env, g=g: env["project"][1][g * tokens_dev : (g + 1) * tokens_dev],
            "dp",
            dp_pairs(-(g // nc), -(g % nc)),
        )

    env = plan.run()

    total = y_sum_p(env, order.index(0))
    for name in arrivals["P"]:
        total = total + env[name].astype(F32)
    proj_grads = total.reshape(proj_count, width, columns)

    score_grads = env["project"][1][:tokens_dev]
    for g in range(1, dp_size):
        score_grads = score_grads + env[f"S{g}"]

    mine = my_rows(env)
    value_grads = jnp.zeros((part_rows, value_width), BF16)
    for g in range(dp_size):
        came = ((x - g // nc) % nx) * nc + (c - g % nc) % nc
        piece = env[f"T{g}"] if g else lax.dynamic_slice_in_dim(mine, dp * part_rows, part_rows, axis=0)
        value_grads = lax.dynamic_update_slice_in_dim(value_grads, piece, came * width, axis=1)
    return (score_grads, value_grads, proj_grads)


def solution(mesh):
    return jax.shard_map(
        local,
        mesh=mesh,
        in_specs=(
            P(("mem", "dp"), None),
            P(("mem", "dp"), None),
            P(("mem", "dp"), None),
            P(("mem", "dp"), None),
            P("mem", None),
            P(None, None, "mem"),
        ),
        out_specs=(P(("mem", "dp"), None), P(("mem", "dp"), None), P(None, "dp", "mem")),
        check_vma=False,
    )
```
